128 devices in a mesh: gx: 32 (over z, y, core), gy: 4 (over x).
Axes of the slice: x: 4, y: 4, z: 4, core: 2. Of those that a mesh axis runs over, the one named last changes fastest.
Arguments:
- state: float32 [5, 512, 1024, 128], P(None, 'gx', 'gy'), may hold values from -6 to 6
- radius: float32 [131072, 128], P(('gx', 'gy')), may hold values from 0.5 to 2
- solute: float32 [131072, 128], P(('gx', 'gy')), may hold values from 0.05 to 0.5
- multiplicity: float32 [131072, 128], P(('gx', 'gy')), may hold values from 0.5 to 4
- block_column: int32 [131072], P(('gx', 'gy')), may hold values from 0 to 4095
- destination: int32 [131072, 1], P(('gx', 'gy')), may hold values from 0 to 8; in each aligned block of 1024 rows (0 to 1023, 1024 to 2047, ...) at most 128 rows name the same one
- live_blocks: int32 [128], P(('gx', 'gy')), may hold values from 1 to 1024, 65536 in all
Outputs:
- new_state: float32 [5, 512, 1024, 128], P(None, 'gx', 'gy')
- new_radius: float32 [147456, 128], P(('gx', 'gy'))
The draws below stay inside these ranges and needn't reach their ends.
Inputs may be any that keep to these rules, and one draw needn't show every extreme that they name: `destination`: on each device at most 128 blocks name one code, and exactly 128 for some code. `live_blocks`: the busiest device is full.
All inputs are finite; a program needn't handle non-finite values.
Results may differ from the reference program's by a relative error of at most 0.0003.
Values sent between devices are 32-bit elements; how exact they have to be, the bound alone decides.
No kernel may reach another device: no remote copies, remote signals or barrier semaphores. Data moves between devices by JAX's collectives and lax.ppermute only.
A program may use at most 256 MiB of HBM per device.

```python
import math
import jax
import jax.numpy as jnp
import numpy as np
from jax import lax

CX = 16
CY = 256
NZ = 128
BLK_DEV = 1024
CAP = 128
ITERS = 4
NX = 512
NY = 1024
N_GX = 32
N_GY = 4
DEVICES = 128


def place_ends(array, stream_key, low, top_value):
    longest = array.shape.index(max(array.shape))
    spots = []
    for shift in (0, 1):
        where = [jax.random.randint(jax.random.fold_in(stream_key, axis), (), 0, length) for axis, length in enumerate(array.shape)]
        where[longest] = (where[longest] + shift) % array.shape[longest]
        spots.append(tuple(where))
    return array.at[spots[0]].set(low).at[spots[1]].set(top_value)


def level_of(key, dims, shards, smallest, top_value):
    factor_of, own = 1.0, jax.random.fold_in(key, 6)
    for dim, parts in shards:
        heights = jnp.exp(jax.random.uniform(jax.random.fold_in(own, dim), (parts,), jnp.float32, smallest / len(shards), top_value / len(shards)))
        factor_of = factor_of * jnp.repeat(heights, dims[dim] // parts).reshape([-1 if axis == dim else 1 for axis in range(len(dims))])
    return factor_of


def length_profile(count, total, limit, skew):
    loads = [(1 << 20) // math.isqrt(standing ** skew) + 1 for standing in range(2, count + 1)]
    rest, holding = total - limit - (count - 1), [1] * (count - 1)
    while rest > 0:
        movable = [i for i in range(count - 1) if holding[i] < limit]
        whole, left = sum([loads[i] for i in movable]), rest
        for i in movable:
            addition = min(limit - holding[i], max(1, left * loads[i] // whole), rest)
            holding[i] = holding[i] + addition
            rest = rest - addition
    return np.array([limit] + holding)


def ragged(own_key, count, total, bound, skew):
    if count == 2:
        one = jax.random.randint(own_key, (), max(1, total - bound), min(bound, total - 1) + 1)
        return jnp.stack([one, total - one])
    lengths = jnp.asarray(length_profile(count, total, bound, skew), jnp.int32)
    pairs = (count - 1) // 2
    source_of, receiver = lengths[1:1 + 2 * pairs:2], lengths[2:2 + 2 * pairs:2]
    room = jnp.minimum(source_of - 1, bound - receiver)
    moved = jax.random.randint(jax.random.fold_in(own_key, 1), (pairs,), 0, 1 << 20) % (room + 1)
    lengths = lengths.at[1:1 + 2 * pairs:2].set(source_of - moved).at[2:2 + 2 * pairs:2].set(receiver + moved)
    return lengths[jax.random.permutation(jax.random.fold_in(own_key, 2), count)]


def deal_out(key, own, number, rows, amount, top, limit, slope):
    ranking = jax.random.permutation(key, amount)
    packed, common = shares(amount, rows * top, limit, slope, True), shares(amount, rows * top, limit, slope, False)
    places = jnp.arange(amount)

    def named(lengths, offset_by):
        used = int((lengths > 0).sum())
        fixed = max(1, used // 4)
        moved = fixed + (places - fixed + offset_by * (used - fixed)) % max(1, amount - fixed)
        return jnp.zeros((amount,), jnp.int32).at[ranking[jnp.where(places < fixed, places, moved)]].set(jnp.asarray(lengths, jnp.int32))

    lengths = jnp.where(number % 4 == 0, named(packed, number // 4), named(common, number - number // 4 - 1))
    mixed = jax.random.permutation(jax.random.fold_in(own, 3), amount)
    giver, sink = mixed[0:amount // 2 * 2:2], mixed[1:amount // 2 * 2:2]
    margin = jnp.minimum(lengths[giver] - 1, limit - lengths[sink]) // 2
    margin = jnp.where((giver == ranking[0]) | (sink == ranking[0]) | (lengths[sink] == 0), 0, jnp.maximum(margin, 0))
    moved = jax.random.randint(jax.random.fold_in(own, 4), (amount // 2,), 0, 1 << 20) % (margin + 1)
    lengths = lengths.at[giver].add(-moved).at[sink].add(moved)
    labels = jnp.searchsorted(jnp.cumsum(lengths), jnp.arange(rows * top), side="right").astype(jnp.int32)
    grid = labels.reshape(top, rows).T
    grid = grid[jax.random.permutation(jax.random.fold_in(own, 1), rows)]
    offset_by = jax.random.randint(jax.random.fold_in(own, 2), (rows, 1), 0, top)
    return jnp.take_along_axis(grid, (jnp.arange(top)[None, :] + offset_by) % top, axis=1)


def shares(number_of, total, reach, slope, full):
    portions = [(1 << 20) // math.isqrt(grade ** slope) + 1 for grade in range(1, number_of + 1)]
    largest = reach if full else min(reach, max(-(-total // number_of), total * portions[0] // sum(portions)))
    least = 1 if total - largest >= number_of - 1 else 0
    counts, rest = [largest] + [least] * (number_of - 1), total - largest - least * (number_of - 1)
    while rest > 0:
        movable = [i for i in range(1, number_of) if counts[i] < largest] or [i for i in range(1, number_of) if counts[i] < reach]
        pool, budget = sum([portions[i] for i in movable]), rest
        for i in movable:
            more = min(reach - counts[i], max(1, budget * portions[i] // pool), rest)
            counts[i] = counts[i] + more
            rest = rest - more
    return np.array(counts)


def normal_values(own_key, extent, spread, most, split=(), kind=jnp.bfloat16):
    result = jax.random.normal(own_key, extent, jnp.float32) * spread
    if len(split) > 0:
        result = level_of(own_key, extent, split, -0.22, 0.18) * result
    return jnp.clip(result, min=-most, max=most).astype(kind)


def setup_inputs(seed: int = 0) -> dict:
    key_list = jax.random.split(jax.random.key(seed), 8)
    state = normal_values(key_list[0], (5, NX, NY, NZ), 1.0, 6.0, ((1, 32), (2, 4)), jnp.float32)
    radius = jnp.clip(jnp.exp(math.log(2.0) - 1.3862944 * jax.random.uniform(key_list[1], (DEVICES * BLK_DEV, NZ), jnp.float32) ** level_of(key_list[1], (DEVICES * BLK_DEV, NZ), ((0, 128),), -0.2, 0.2)), 0.5, 2.0)
    solute = jnp.clip(jnp.exp(math.log(0.5) - 2.3025851 * jax.random.uniform(key_list[2], (DEVICES * BLK_DEV, NZ), jnp.float32) ** level_of(key_list[2], (DEVICES * BLK_DEV, NZ), ((0, 128),), -0.2, 0.2)), 0.05, 0.5)
    multiplicity = jnp.clip(jnp.exp(math.log(4.0) - 2.0794415 * jax.random.uniform(key_list[3], (DEVICES * BLK_DEV, NZ), jnp.float32) ** level_of(key_list[3], (DEVICES * BLK_DEV, NZ), ((0, 128),), -0.2, 0.2)), 0.5, 4.0)
    block_column = place_ends(jax.random.randint(key_list[4], (DEVICES * BLK_DEV,), 0, CX * CY), jax.random.fold_in(key_list[4], 1), 0, (CX * CY) - 1).astype(jnp.int32)
    destination_keys = jax.random.split(jax.random.fold_in(key_list[5], 1), (DEVICES * BLK_DEV) // BLK_DEV)
    destination_turns = jax.random.permutation(jax.random.fold_in(key_list[5], 3), (DEVICES * BLK_DEV) // BLK_DEV)
    destination = jax.vmap(lambda own, number: deal_out(jax.random.fold_in(key_list[5], 2), own, number, BLK_DEV, 9, 1, CAP, 2))(destination_keys, destination_turns).reshape((DEVICES * BLK_DEV, 1))
    live_blocks = ragged(key_list[6], DEVICES, DEVICES * BLK_DEV // 2, BLK_DEV, 2).astype(jnp.int32)
    return dict(state=state, radius=radius, solute=solute, multiplicity=multiplicity, block_column=block_column, destination=destination, live_blocks=live_blocks)


smag_coef = 0.02
buoyancy_coef = 0.5
growth_coef = 0.6
curvature_coef = 0.1
solute_coef = 0.3
floor_square = 0.04
condense_coef = 0.5
latent_coef = 0.8
epsilon = 1e-06

def dynamics(state):
    upper = jnp.concatenate([state[..., 1:], state[..., -1:]], axis=3)
    lower = jnp.concatenate([state[..., :1], state[..., :-1]], axis=3)
    east = jnp.roll(state, -1, axis=1)
    west = jnp.roll(state, 1, axis=1)
    north = jnp.roll(state, -1, axis=2)
    south = jnp.roll(state, 1, axis=2)
    dxs = (east - west) * 0.5
    dys = (north - south) * 0.5
    dzs = (upper - lower) * 0.5
    laplace = east + west + north + south + upper + lower - 6.0 * state
    strain = 2.0 * (dxs[0] * dxs[0] + dys[1] * dys[1] + dzs[2] * dzs[2])
    strain = strain + (dys[0] + dxs[1]) ** 2 + (dzs[0] + dxs[2]) ** 2 + (dzs[1] + dys[2]) ** 2
    viscosity = smag_coef * jnp.sqrt(strain + epsilon)
    fresh = state + viscosity[None] * laplace
    return fresh.at[2].add(buoyancy_coef * state[3])

def pack_blocks(rad, sol, mul, col, code, count):
    blocks = rad.shape[0]
    cap = blocks // 8
    live = jnp.arange(blocks, dtype=jnp.int32) < count
    hit = ((code[:, None] == jnp.arange(9, dtype=jnp.int32)[None, :]) & live[:, None]).astype(jnp.int32)
    rank = jnp.cumsum(hit, axis=0) - hit
    slot = lax.optimization_barrier(jnp.sum(rank * hit, axis=1))
    place = jnp.where(live, code * cap + slot, 9 * cap).astype(jnp.int32)

    def put(values):
        empty = jnp.zeros((10 * cap,) + values.shape[1:], jnp.float32)
        return empty.at[place].set(values)[:9 * cap]
    return (put(rad), put(sol), put(mul), put(col.astype(jnp.float32)))

def condense(sat, rad, sol, mul):
    alive = mul > 0.0
    start = jnp.where(alive, rad, 1.0)
    value = start
    for step in range(ITERS):
        inside = start * start + growth_coef * (sat - curvature_coef / value + solute_coef * sol / (value * value * value))
        value = jnp.sqrt(jnp.maximum(inside, floor_square))
    condensed = mul * (value * value * value - start * start * start)
    return (jnp.where(alive, value, 0.0), condensed)

def reference(state, radius, solute, multiplicity, block_column, destination, live_blocks):
    fresh = dynamics(state)
    devices = N_GX * N_GY
    shape3 = (devices, BLK_DEV, NZ)
    bufr, bufs, bufm, bufc = jax.vmap(pack_blocks)(radius.reshape(shape3), solute.reshape(shape3), multiplicity.reshape(shape3), block_column.reshape(devices, BLK_DEV), destination.reshape(devices, BLK_DEV), live_blocks)
    device = jnp.arange(devices, dtype=jnp.int32)
    tilex = device // N_GY
    tiley = device % N_GY
    codes = jnp.arange(9, dtype=jnp.int32)
    shiftx = codes // 3 - 1
    shifty = codes % 3 - 1
    source = (tilex[:, None] - shiftx[None, :]) % N_GX * N_GY + (tiley[:, None] - shifty[None, :]) % N_GY
    which = codes[None, :]
    recv_r = bufr.reshape(devices, 9, CAP, NZ)[source, which]
    recv_s = bufs.reshape(devices, 9, CAP, NZ)[source, which]
    recv_m = bufm.reshape(devices, 9, CAP, NZ)[source, which]
    recv_c = bufc.reshape(devices, 9, CAP)[source, which].astype(jnp.int32)
    cellx = (tilex[:, None, None] * CX + recv_c // CY).astype(jnp.int32)
    celly = (tiley[:, None, None] * CY + recv_c % CY).astype(jnp.int32)
    field = fresh[4] - 0.5 * fresh[3]
    sat = field[cellx, celly]
    value, condensed = condense(sat, recv_r, recv_s, recv_m)
    levels = jnp.arange(NZ, dtype=jnp.int32)
    total = jnp.zeros((NX, NY, NZ), jnp.float32).at[cellx[..., None], celly[..., None], levels].add(condensed)
    vapour = fresh[4] - condense_coef * total
    buoyancy = fresh[3] + latent_coef * total
    new_state = jnp.stack([fresh[0], fresh[1], fresh[2], buoyancy, vapour])
    return (new_state, value.reshape(devices * 9 * CAP, NZ))
```

```python
import functools

import jax
import jax.numpy as jnp
from jax import lax
from jax.experimental import pallas as pl
from jax.experimental.pallas import tpu as pltpu
from jax.sharding import PartitionSpec as P

ITERS = 4
CODES = 9
OWN = 4

smag_coef = 0.02
buoyancy_coef = 0.5
growth_coef = 0.6
curvature_coef = 0.1
solute_coef = 0.3
floor_square = 0.04
condense_coef = 0.5
latent_coef = 0.8
epsilon = 1e-06

f32 = jnp.float32
bf16 = jnp.bfloat16
i32 = jnp.int32
HBM = pl.BlockSpec(memory_space=pl.ANY)
VMEM = pl.BlockSpec(memory_space=pltpu.VMEM)
SMEM = pl.BlockSpec(memory_space=pltpu.SMEM)


def iota(shape, dim):
    return lax.broadcasted_iota(i32, shape, dim)


def halves(value):
    high = value.astype(bf16)
    low = (value - high.astype(f32)).astype(bf16)
    return high, low


def pack_kernel(cap, live_ref, code_ref, col_ref, rad_ref, sol_ref, mul_ref, *rest):
    outs = rest[:CODES]
    onehot, values = rest[CODES:]
    rows, lanes = code_ref.shape
    code = code_ref[...]
    live = iota((rows, lanes), 0) * lanes + iota((rows, lanes), 1) < live_ref[0]
    hits = [jnp.where((code == k) & live, 1.0, 0.0) for k in range(CODES)]
    hit = jnp.concatenate(hits, axis=0)
    wide = iota((lanes, 2 * lanes), 1)
    before = jnp.where((iota((lanes, 2 * lanes), 0) < wide) | (wide >= lanes), 1.0, 0.0)
    inside = jnp.dot(hit, before, preferred_element_type=f32)
    high = CODES * rows
    a, b = iota((high, high), 0), iota((high, high), 1)
    above = jnp.where((a // rows == b // rows) & (b < a), 1.0, 0.0)
    rank = inside[:, :lanes] + jnp.dot(above, inside[:, lanes:], preferred_element_type=f32)
    place = jnp.where(hit > 0.0, rank, -1.0).astype(i32)
    slot = iota((cap, lanes), 0)
    for k in range(CODES):
        for row in range(rows):
            spot = place[k * rows + row : k * rows + row + 1, :]
            onehot[k * cap : (k + 1) * cap, row * lanes : (row + 1) * lanes] = jnp.where(
                slot == spot, 1.0, 0.0
            ).astype(bf16)
    for part, ref in enumerate((rad_ref, sol_ref, mul_ref)):
        top, low = halves(ref[...])
        values[:, part * 128 : part * 128 + 128] = top
        values[:, 384 + part * 128 : 512 + part * 128] = low
    moved = jnp.dot(onehot[...], values[...], preferred_element_type=f32)
    moved = moved[:, :384] + moved[:, 384:]
    col = col_ref[...]
    coarse = (col // 16 * 16).astype(f32)
    fine = (col % 16).astype(f32)
    flat = jnp.concatenate(
        [
            jnp.concatenate([item[row : row + 1] for row in range(rows)], axis=1)
            for item in (coarse, fine)
        ]
        + [jnp.zeros((6, rows * lanes), f32)],
        axis=0,
    ).astype(bf16)
    for k in range(CODES):
        for part in range(3):
            outs[k][part * cap : (part + 1) * cap, :] = moved[
                k * cap : (k + 1) * cap, part * 128 : (part + 1) * 128
            ]
        cols = lax.dot_general(
            flat,
            onehot[k * cap : (k + 1) * cap, :],
            (((1,), (1,)), ((), ())),
            preferred_element_type=f32,
        )
        outs[k][3 * cap : 3 * cap + 8, :] = jnp.broadcast_to(cols[0:1] + cols[1:2], (8, 128))


def pack_blocks(rad, sol, mul, col, code, count):
    blocks = rad.shape[0]
    cap = blocks // 8
    rows = blocks // 128
    return pl.pallas_call(
        functools.partial(pack_kernel, cap),
        out_shape=[jax.ShapeDtypeStruct((3 * cap + 8, 128), f32)] * CODES,
        in_specs=[SMEM] + [VMEM] * 5,
        out_specs=[VMEM] * CODES,
        scratch_shapes=[
            pltpu.VMEM((CODES * cap, blocks), bf16),
            pltpu.VMEM((blocks, 768), bf16),
        ],
        compiler_params=pltpu.CompilerParams(vmem_limit_bytes=40 << 20),
        cost_estimate=pl.CostEstimate(flops=2_000_000_000, bytes_accessed=4 << 20, transcendentals=0),
        name="pack",
    )(count, code.reshape(rows, 128), col.reshape(rows, 128), rad, sol, mul)


PAD = 8
CHUNK = 16


def plane_step(here, west, east, put):
    ny = 256

    def chunk(step, carry):
        base = PAD + step * CHUNK
        lane = iota((CHUNK, 128), 1)

        def around(f):
            c = here(f, base, 0)
            up = jnp.where(lane == 127, c, pltpu.roll(c, 127, 1))
            low = jnp.where(lane == 0, c, pltpu.roll(c, 1, 1))
            n = here(f, base, 1)
            s = here(f, base, -1)
            e = east(f, base)
            w = west(f, base)
            return c, e, w, n, s, up, low

        def lap(parts):
            c, e, w, n, s, up, low = parts
            return e + w + n + s + up + low - 6.0 * c

        def slopes(parts):
            c, e, w, n, s, up, low = parts
            return e - w, n - s, up - low

        pu, pv, pw = around(0), around(1), around(2)
        du, dv, dw = slopes(pu), slopes(pv), slopes(pw)
        strain = 2.0 * (du[0] * du[0] + dv[1] * dv[1] + dw[2] * dw[2])
        uv = du[1] + dv[0]
        uw = du[2] + dw[0]
        vw = dv[2] + dw[1]
        strain = strain + uv * uv + uw * uw + vw * vw
        visc = smag_coef * jnp.sqrt(0.25 * strain + epsilon)
        row = step * CHUNK
        put(0, row, pu[0] + visc * lap(pu))
        put(1, row, pv[0] + visc * lap(pv))
        pb = around(3)
        put(2, row, pw[0] + visc * lap(pw) + buoyancy_coef * pb[0])
        fb = pb[0] + visc * lap(pb)
        put(3, row, fb)
        pq = around(4)
        fq = pq[0] + visc * lap(pq)
        put(4, row, fq)
        put(5, row, fq - 0.5 * fb)
        return carry

    lax.fori_loop(0, ny // CHUNK, chunk, 0)


def inner_kernel(state, south, north, new, sat, planes, fresh, sat_out, in_sem, out_sem, sat_sem):
    nx, ny = state.shape[1], state.shape[2]

    def fetch(x):
        return pltpu.make_async_copy(
            state.at[:, x], planes.at[:, x, pl.ds(PAD, ny), :], in_sem.at[x]
        )

    def store(x):
        return pltpu.make_async_copy(fresh.at[:, x], new.at[:, x], out_sem.at[x])

    def store_sat(x):
        return pltpu.make_async_copy(
            sat_out.at[pl.ds(x * ny, ny), :], sat.at[pl.ds(x * ny, ny), :], sat_sem.at[x]
        )

    for x in range(nx):
        fetch(x).start()
    for f in range(5):
        for x in range(1, nx - 1):
            planes[f, x, PAD - 1 : PAD, :] = south[f, x : x + 1, :]
            planes[f, x, PAD + ny : PAD + ny + 1, :] = north[f, x : x + 1, :]
    fetch(0).wait()
    fetch(1).wait()

    def body(x, carry):
        fetch(x + 1).wait()

        def here(f, base, shift):
            return planes[f, x, pl.ds(base + shift, CHUNK), :]

        def west(f, base):
            return planes[f, x - 1, pl.ds(base, CHUNK), :]

        def east(f, base):
            return planes[f, x + 1, pl.ds(base, CHUNK), :]

        def put(f, row, value):
            if f == 5:
                sat_out[pl.ds(x * ny + row, CHUNK), :] = value
            else:
                fresh[f, x, pl.ds(row, CHUNK), :] = value

        plane_step(here, west, east, put)
        store(x).start()
        store_sat(x).start()
        return carry

    lax.fori_loop(1, nx - 1, body, 0)
    for x in range(1, nx - 1):
        store(x).wait()
        store_sat(x).wait()


def rim_kernel(
    state, south, north, left, right, new_in, sat_in, new, sat, planes, fresh, sat_out, in_sem, out_sem, sat_sem
):
    nx, ny = state.shape[1], state.shape[2]
    sources = (left.at[:, 0], state.at[:, 0], state.at[:, 1], state.at[:, nx - 2], state.at[:, nx - 1], right.at[:, 0])
    copies = [
        pltpu.make_async_copy(source, planes.at[:, slot, pl.ds(PAD, ny), :], in_sem.at[slot])
        for slot, source in enumerate(sources)
    ]
    for copy in copies:
        copy.start()
    for f in range(5):
        for slot, x in ((1, 0), (4, nx - 1)):
            planes[f, slot, PAD - 1 : PAD, :] = south[f, x : x + 1, :]
            planes[f, slot, PAD + ny : PAD + ny + 1, :] = north[f, x : x + 1, :]
    waits = []
    for side, (slot, x) in enumerate(((1, 0), (4, nx - 1))):
        for copy in copies[3 * side : 3 * side + 3]:
            copy.wait()

        def here(f, base, shift, slot=slot):
            return planes[f, slot, pl.ds(base + shift, CHUNK), :]

        def west(f, base, slot=slot):
            return planes[f, slot - 1, pl.ds(base, CHUNK), :]

        def east(f, base, slot=slot):
            return planes[f, slot + 1, pl.ds(base, CHUNK), :]

        def put(f, row, value, side=side):
            if f == 5:
                sat_out[side, pl.ds(row, CHUNK), :] = value
            else:
                fresh[f, side, pl.ds(row, CHUNK), :] = value

        plane_step(here, west, east, put)
        one = pltpu.make_async_copy(fresh.at[:, side], new.at[:, x], out_sem.at[side])
        two = pltpu.make_async_copy(sat_out.at[side], sat.at[pl.ds(x * ny, ny), :], sat_sem.at[side])
        one.start()
        two.start()
        waits += [one, two]
    for copy in waits:
        copy.wait()


def inner_planes(state, south, north):
    _, nx, ny, nz = state.shape
    return pl.pallas_call(
        inner_kernel,
        out_shape=[
            jax.ShapeDtypeStruct(state.shape, f32),
            jax.ShapeDtypeStruct((nx * ny, nz), f32),
        ],
        in_specs=[HBM, VMEM, VMEM],
        out_specs=[HBM, HBM],
        scratch_shapes=[
            pltpu.VMEM((5, nx, ny + 2 * PAD, nz), f32),
            pltpu.VMEM((5, nx, ny, nz), f32),
            pltpu.VMEM((nx * ny, nz), f32),
            pltpu.SemaphoreType.DMA((nx,)),
            pltpu.SemaphoreType.DMA((nx,)),
            pltpu.SemaphoreType.DMA((nx,)),
        ],
        compiler_params=pltpu.CompilerParams(vmem_limit_bytes=40 << 20),
        cost_estimate=pl.CostEstimate(flops=60_000_000, bytes_accessed=24 << 20, transcendentals=0),
        name="inner",
    )(state, south, north)


def rim_planes(state, south, north, left, right, new, sat):
    _, nx, ny, nz = state.shape
    return pl.pallas_call(
        rim_kernel,
        out_shape=[
            jax.ShapeDtypeStruct(state.shape, f32),
            jax.ShapeDtypeStruct((nx * ny, nz), f32),
        ],
        in_specs=[HBM, VMEM, VMEM] + [HBM] * 4,
        out_specs=[HBM, HBM],
        input_output_aliases={5: 0, 6: 1},
        scratch_shapes=[
            pltpu.VMEM((5, 6, ny + 2 * PAD, nz), f32),
            pltpu.VMEM((5, 2, ny, nz), f32),
            pltpu.VMEM((2, ny, nz), f32),
            pltpu.SemaphoreType.DMA((6,)),
            pltpu.SemaphoreType.DMA((2,)),
            pltpu.SemaphoreType.DMA((2,)),
        ],
        compiler_params=pltpu.CompilerParams(vmem_limit_bytes=24 << 20),
        cost_estimate=pl.CostEstimate(flops=8_000_000, bytes_accessed=6 << 20, transcendentals=0),
        name="rim",
    )(state, south, north, left, right, new, sat)


SUMS = 3


def grow_kernel(cap, *refs):
    bufs = refs[:CODES]
    sat_hbm, new_in, radius, new = refs[CODES : CODES + 4]
    sat, near, total_refs, fields, cols_v, cols_s = (
        refs[CODES + 4],
        refs[CODES + 5],
        refs[CODES + 6 : CODES + 6 + SUMS],
        refs[CODES + 6 + SUMS],
        refs[CODES + 7 + SUMS],
        refs[CODES + 8 + SUMS],
    )
    sat_sem, field_sem, col_sem, out_sem = refs[CODES + 9 + SUMS :]
    nx, ny = new.shape[1], new.shape[2]
    get_sat = pltpu.make_async_copy(sat_hbm, sat, sat_sem)
    get_sat.start()
    for k in range(CODES):
        cols_v[k : k + 1, :] = bufs[k][3 * cap : 3 * cap + 1, :].astype(i32)
    get_cols = pltpu.make_async_copy(cols_v, cols_s, col_sem)
    get_cols.start()
    get_fields = pltpu.make_async_copy(new_in.at[pl.ds(3, 2)], fields, field_sem)
    get_fields.start()
    for total in total_refs:
        total[...] = jnp.zeros_like(total)
    get_cols.wait()
    get_sat.wait()
    UN = 8
    for k in range(CODES):
        def gather(step, carry, k=k):
            for u in range(UN):
                j = step * UN + u
                near[pl.ds(k * cap + j, 1), :] = sat[pl.ds(cols_s[k, j], 1), :]
            return carry

        lax.fori_loop(0, cap // UN, gather, 0)
    for k in range(CODES):
        def grow(step, carry, k=k):
            at = step * 16
            rad = bufs[k][pl.ds(at, 16), :]
            sol = bufs[k][pl.ds(cap + at, 16), :]
            mul = bufs[k][pl.ds(2 * cap + at, 16), :]
            here = near[pl.ds(k * cap + at, 16), :]
            alive = mul > 0.0
            start = jnp.where(alive, rad, 1.0)
            square = start * start
            base = square + growth_coef * here
            sol = (growth_coef * solute_coef) * sol
            inv = 1.0 / start
            for _ in range(ITERS):
                inside = base + inv * (sol * (inv * inv) - growth_coef * curvature_coef)
                inside = jnp.maximum(inside, floor_square)
                inv = lax.rsqrt(inside)
            value = inside * inv
            radius[pl.ds(k * cap + at, 16), :] = jnp.where(alive, value, 0.0)
            near[pl.ds(k * cap + at, 16), :] = mul * (value * inside - start * square)
            return carry

        lax.fori_loop(0, cap // 16, grow, 0)
    for k in range(0, CODES, SUMS):
        def scatter(step, carry, k=k):
            for u in range(4):
                j = step * 4 + u
                for g in range(SUMS):
                    c = cols_s[k + g, j]
                    total_refs[g][pl.ds(c, 1), :] += near[pl.ds((k + g) * cap + j, 1), :]
            return carry

        lax.fori_loop(0, cap // 4, scatter, 0)
    get_fields.wait()

    def put(x):
        return pltpu.make_async_copy(fields.at[:, x], new.at[pl.ds(3, 2), x], out_sem.at[x])

    def final(x, carry):
        def rows(step, c2):
            at = step * 32
            tot = total_refs[0][pl.ds(x * ny + at, 32), :]
            for g in range(1, SUMS):
                tot = tot + total_refs[g][pl.ds(x * ny + at, 32), :]
            fields[0, x, pl.ds(at, 32), :] += latent_coef * tot
            fields[1, x, pl.ds(at, 32), :] -= condense_coef * tot
            return c2

        lax.fori_loop(0, ny // 32, rows, 0)
        put(x).start()
        return carry

    lax.fori_loop(0, nx, final, 0)
    for x in range(nx):
        put(x).wait()


def grow_blocks(bufs, sat, new):
    _, nx, ny, nz = new.shape
    cap = (bufs[0].shape[0] - 8) // 3
    return pl.pallas_call(
        functools.partial(grow_kernel, cap),
        out_shape=[
            jax.ShapeDtypeStruct((CODES * cap, nz), f32),
            jax.ShapeDtypeStruct(new.shape, f32),
        ],
        in_specs=[VMEM] * CODES + [HBM, HBM],
        out_specs=[VMEM, HBM],
        input_output_aliases={CODES + 1: 1},
        scratch_shapes=[
            pltpu.VMEM((nx * ny, nz), f32),
            pltpu.VMEM((CODES * cap, nz), f32),
        ]
        + [pltpu.VMEM((nx * ny, nz), f32) for _ in range(SUMS)]
        + [
            pltpu.VMEM((2, nx, ny, nz), f32),
            pltpu.VMEM((16, 128), i32),
            pltpu.SMEM((16, 128), i32),
            pltpu.SemaphoreType.DMA,
            pltpu.SemaphoreType.DMA,
            pltpu.SemaphoreType.DMA,
            pltpu.SemaphoreType.DMA((nx,)),
        ],
        compiler_params=pltpu.CompilerParams(vmem_limit_bytes=32 << 20),
        cost_estimate=pl.CostEstimate(flops=20_000_000, bytes_accessed=12 << 20, transcendentals=0),
        name="grow",
    )(*bufs, sat, new)


def moved(value, dx, dy):
    nx, ny = lax.axis_size("gx"), lax.axis_size("gy")
    pairs = [
        (tx * ny + ty, (tx + dx) % nx * ny + (ty + dy) % ny) for tx in range(nx) for ty in range(ny)
    ]
    return lax.ppermute(value, ("gx", "gy"), pairs)


def on_device(state, radius, solute, multiplicity, block_column, destination, live_blocks):
    left = moved(state[:, -1:], 1, 0)
    right = moved(state[:, :1], -1, 0)
    south = moved(state[:, :, -1], 0, 1)
    north = moved(state[:, :, 0], 0, -1)
    packed = pack_blocks(radius, solute, multiplicity, block_column, destination, live_blocks)
    received = [
        packed[k] if k == OWN else moved(packed[k], k // 3 - 1, k % 3 - 1) for k in range(CODES)
    ]
    new, sat = inner_planes(state, south, north)
    new, sat = rim_planes(state, south, north, left, right, new, sat)
    value, new = grow_blocks(received, sat, new)
    return new, value


def solution(mesh):
    placed = (
        P(None, "gx", "gy", None),
        P(("gx", "gy"), None),
        P(("gx", "gy"), None),
        P(("gx", "gy"), None),
        P(("gx", "gy")),
        P(("gx", "gy"), None),
        P(("gx", "gy")),
    )
    return jax.shard_map(
        on_device,
        mesh=mesh,
        in_specs=placed,
        out_specs=(P(None, "gx", "gy", None), P(("gx", "gy"), None)),
        check_vma=False,
    )
```

```python
import functools

import jax
import jax.numpy as jnp
from jax import lax
from jax.experimental import pallas as pl
from jax.experimental.pallas import tpu as pltpu
from jax.sharding import PartitionSpec as P

ITERS = 4
CODES = 9
OWN = 4

smag_coef = 0.02
buoyancy_coef = 0.5
growth_coef = 0.6
curvature_coef = 0.1
solute_coef = 0.3
floor_square = 0.04
condense_coef = 0.5
latent_coef = 0.8
epsilon = 1e-06

f32 = jnp.float32
bf16 = jnp.bfloat16
i32 = jnp.int32
HBM = pl.BlockSpec(memory_space=pltpu.HBM)
VMEM = pl.BlockSpec(memory_space=pltpu.VMEM)
SMEM = pl.BlockSpec(memory_space=pltpu.SMEM)


def iota(shape, dim):
    return lax.broadcasted_iota(i32, shape, dim)


def halves(value):
    high = value.astype(bf16)
    low = (value - high.astype(f32)).astype(bf16)
    return high, low


FIRST = ((-1, 0, 1, 0), (1, 0, 7, 8), (0, -1, 3, 6), (0, 1, 5, 2))
SECOND = ((0, -1, 0), (0, 1, 8), (1, 0, 6), (-1, 0, 2))


def parcel_rows(cap):
    return 3 * cap + 8


def pack_kernel(
    cap, live_ref, code_hbm, col_hbm, rad_hbm, sol_hbm, mul_hbm, state,
    west_out, east_out, south_out, north_out, own_out,
    code_ref, col_ref, drops, edges, onehot, values, sems,
):
    nx, ny = state.shape[1], state.shape[2]
    tops = (5 * ny, 5 * ny, 5 * nx, 5 * nx)
    sides = (west_out, east_out, south_out, north_out)
    small = [
        pltpu.make_async_copy(code_hbm, code_ref, sems.at[0]),
        pltpu.make_async_copy(col_hbm, col_ref, sems.at[1]),
    ]
    big = [
        pltpu.make_async_copy(ref, drops.at[part], sems.at[2 + part])
        for part, ref in enumerate((rad_hbm, sol_hbm, mul_hbm))
    ]
    edge = [
        pltpu.make_async_copy(state.at[:, :, pl.ds(0, 8), :], edges.at[0], sems.at[5]),
        pltpu.make_async_copy(state.at[:, :, pl.ds(ny - 8, 8), :], edges.at[1], sems.at[6]),
    ]
    rims = [
        pltpu.make_async_copy(
            state.at[f, x], side.at[pl.ds(f * ny, ny), :], sems.at[7 + 5 * which + f]
        )
        for which, (side, x) in enumerate(((west_out, 0), (east_out, nx - 1)))
        for f in range(5)
    ]
    for copy in small + big + edge + rims:
        copy.start()
    for copy in small:
        copy.wait()
    rows, lanes = code_ref.shape
    code = code_ref[...]
    live = iota((rows, lanes), 0) * lanes + iota((rows, lanes), 1) < live_ref[0]
    hits = [jnp.where((code == k) & live, 1.0, 0.0) for k in range(CODES)]
    hit = jnp.concatenate(hits, axis=0)
    wide = iota((lanes, 2 * lanes), 1)
    before = jnp.where((iota((lanes, 2 * lanes), 0) < wide) | (wide >= lanes), 1.0, 0.0)
    inside = jnp.dot(hit, before, preferred_element_type=f32)
    high = CODES * rows
    a, b = iota((high, high), 0), iota((high, high), 1)
    above = jnp.where((a // rows == b // rows) & (b < a), 1.0, 0.0)
    rank = inside[:, :lanes] + jnp.dot(above, inside[:, lanes:], preferred_element_type=f32)
    place = jnp.where(hit > 0.0, rank, -1.0).astype(i32)
    slot = iota((cap, lanes), 0)
    for k in range(CODES):
        for row in range(rows):
            spot = place[k * rows + row : k * rows + row + 1, :]
            onehot[k * cap : (k + 1) * cap, row * lanes : (row + 1) * lanes] = jnp.where(
                slot == spot, 1.0, 0.0
            ).astype(bf16)
    for part in range(3):
        big[part].wait()
        top, low = halves(drops[part])
        values[:, part * 128 : part * 128 + 128] = top
        values[:, 384 + part * 128 : 512 + part * 128] = low
    moved = jnp.dot(onehot[...], values[...], preferred_element_type=f32)
    moved = moved[:, :384] + moved[:, 384:]
    col = col_ref[...]
    coarse = (col // 16 * 16).astype(f32)
    fine = (col % 16).astype(f32)
    flat = jnp.concatenate(
        [
            jnp.concatenate([item[row : row + 1] for row in range(rows)], axis=1)
            for item in (coarse, fine)
        ]
        + [jnp.zeros((6, rows * lanes), f32)],
        axis=0,
    ).astype(bf16)
    spots = {OWN: (own_out, 0)}
    for side, top, (_, _, end, diagonal) in zip(sides, tops, FIRST):
        spots[end] = (side, top)
        spots[diagonal] = (side, top + parcel_rows(cap))
    for k in range(CODES):
        ref, at = spots[k]
        for part in range(3):
            ref[at + part * cap : at + (part + 1) * cap, :] = moved[
                k * cap : (k + 1) * cap, part * 128 : (part + 1) * 128
            ]
        cols = lax.dot_general(
            flat,
            onehot[k * cap : (k + 1) * cap, :],
            (((1,), (1,)), ((), ())),
            preferred_element_type=f32,
        )
        ref[at + 3 * cap : at + 3 * cap + 8, :] = jnp.broadcast_to(cols[0:1] + cols[1:2], (8, 128))
    for copy in edge:
        copy.wait()
    for f in range(5):
        for x in range(nx):
            at = f * nx + x
            south_out[at : at + 1, :] = edges[0, f, x, 0:1, :]
            north_out[at : at + 1, :] = edges[1, f, x, 7:8, :]
    for copy in rims:
        copy.wait()


def pack_blocks(rad, sol, mul, col, code, count, state):
    blocks = rad.shape[0]
    cap = blocks // 8
    rows = blocks // 128
    _, nx, ny, nz = state.shape
    one = parcel_rows(cap)
    heights = [5 * ny + 2 * one] * 2 + [5 * nx + 2 * one] * 2 + [one]
    return pl.pallas_call(
        functools.partial(pack_kernel, cap),
        out_shape=[jax.ShapeDtypeStruct((height, nz), f32) for height in heights],
        in_specs=[SMEM] + [HBM] * 6,
        out_specs=[VMEM] * 5,
        scratch_shapes=[
            pltpu.VMEM((rows, 128), i32),
            pltpu.VMEM((rows, 128), i32),
            pltpu.VMEM((3, blocks, nz), f32),
            pltpu.VMEM((2, 5, nx, 8, nz), f32),
            pltpu.VMEM((CODES * cap, blocks), bf16),
            pltpu.VMEM((blocks, 6 * nz), bf16),
            pltpu.SemaphoreType.DMA((17,)),
        ],
        compiler_params=pltpu.CompilerParams(vmem_limit_bytes=60 << 20),
        cost_estimate=pl.CostEstimate(flops=2_000_000_000, bytes_accessed=4 << 20, transcendentals=0),
        name="pack",
    )(count, code.reshape(rows, 128), col.reshape(rows, 128), rad, sol, mul, state)


def step_rows(here, west, east, put):
    lane = iota((8, 128), 1)

    def around(f):
        c = here(f, 0)
        up = jnp.where(lane == 127, c, pltpu.roll(c, 127, 1))
        low = jnp.where(lane == 0, c, pltpu.roll(c, 1, 1))
        return c, east(f), west(f), here(f, 1), here(f, -1), up, low

    def lap(parts):
        c, e, w, n, s, up, low = parts
        return e + w + n + s + up + low - 6.0 * c

    def slopes(parts):
        c, e, w, n, s, up, low = parts
        return e - w, n - s, up - low

    pu, pv, pw = around(0), around(1), around(2)
    du, dv, dw = slopes(pu), slopes(pv), slopes(pw)
    strain = 2.0 * (du[0] * du[0] + dv[1] * dv[1] + dw[2] * dw[2])
    uv = du[1] + dv[0]
    uw = du[2] + dw[0]
    vw = dv[2] + dw[1]
    strain = strain + uv * uv + uw * uw + vw * vw
    visc = smag_coef * jnp.sqrt(0.25 * strain + epsilon)
    put(0, pu[0] + visc * lap(pu))
    put(1, pv[0] + visc * lap(pv))
    pb = around(3)
    put(2, pw[0] + visc * lap(pw) + buoyancy_coef * pb[0])
    fb = pb[0] + visc * lap(pb)
    put(3, fb)
    pq = around(4)
    fq = pq[0] + visc * lap(pq)
    put(4, fq)
    put(5, fq - 0.5 * fb)


def inner_kernel(state, new, sat, planes, fresh, sat_out, in_sem, out_sem, sat_sem):
    nx, ny = state.shape[1], state.shape[2]
    inside = pl.ds(8, ny - 16)

    def fetch(x):
        return pltpu.make_async_copy(state.at[:, x], planes.at[:, x], in_sem.at[x])

    def store(x):
        return pltpu.make_async_copy(
            fresh.at[:, x, inside, :], new.at[:, x, inside, :], out_sem.at[x]
        )

    def store_sat(x):
        rows = pl.ds(x * ny + 8, ny - 16)
        return pltpu.make_async_copy(sat_out.at[rows, :], sat.at[rows, :], sat_sem.at[x])

    for x in range(nx):
        fetch(x).start()
    fetch(0).wait()
    fetch(1).wait()

    def body(x, carry):
        fetch(x + 1).wait()
        for base in range(8, ny - 8, 8):

            def here(f, shift, base=base):
                return planes[f, x, base + shift : base + shift + 8, :]

            def west(f, base=base):
                return planes[f, x - 1, base : base + 8, :]

            def east(f, base=base):
                return planes[f, x + 1, base : base + 8, :]

            def put(f, value, base=base):
                if f == 5:
                    sat_out[pl.ds(pl.multiple_of(x * ny + base, 8), 8), :] = value
                else:
                    fresh[f, x, base : base + 8, :] = value

            step_rows(here, west, east, put)
        store(x).start()
        store_sat(x).start()
        return carry

    lax.fori_loop(1, nx - 1, body, 0)
    for x in range(1, nx - 1):
        store(x).wait()
        store_sat(x).wait()


def rim_kernel(
    state, left, right, south, north, new_in, sat_in, new, sat,
    planes, fresh, slabs, edges, sat_out, sat_edge, in_sem, slab_sem, out_sem,
):
    nx, ny = state.shape[1], state.shape[2]
    slab_in = [
        pltpu.make_async_copy(
            state.at[:, :, pl.ds(0, 16), :], slabs.at[0, :, :, pl.ds(8, 16), :], slab_sem.at[0]
        ),
        pltpu.make_async_copy(
            state.at[:, :, pl.ds(ny - 16, 16), :], slabs.at[1, :, :, pl.ds(0, 16), :], slab_sem.at[1]
        ),
    ]
    fetch = [
        pltpu.make_async_copy(state.at[:, x], planes.at[:, slot], in_sem.at[slot])
        for slot, x in enumerate((0, 1, nx - 2, nx - 1))
    ]
    for copy in slab_in + fetch:
        copy.start()
    for f in range(5):
        for x in range(nx):
            at = f * nx + x
            slabs[0, f, x, 7:8, :] = south[at : at + 1, :]
            slabs[1, f, x, 16:17, :] = north[at : at + 1, :]
    waits = []
    sems = iter(range(16))

    def send(source, target):
        copy = pltpu.make_async_copy(source, target, out_sem.at[next(sems)])
        copy.start()
        waits.append(copy)

    for copy in slab_in:
        copy.wait()

    def edge_rows(x, west_of, east_of):
        for side in range(2):

            def here(f, shift, side=side):
                return slabs[side, f, x, 8 + shift : 16 + shift, :]

            def put(f, value, side=side):
                if f == 5:
                    sat_edge[side, x] = value
                else:
                    edges[side, f, x] = value

            step_rows(here, functools.partial(west_of, side), functools.partial(east_of, side), put)

    def beside(x):
        return lambda side, f: slabs[side, f, x, 8:16, :]

    def halo(ref):
        return lambda side, f: ref[f * ny + side * (ny - 8) : f * ny + side * (ny - 8) + 8, :]

    edge_rows(0, halo(left), beside(1))
    edge_rows(nx - 1, beside(nx - 2), halo(right))

    def pair(step, carry):
        for part in range(2):
            x = 1 + step * 2 + part
            edge_rows(x, beside(x - 1), beside(x + 1))
        return carry

    lax.fori_loop(0, (nx - 2) // 2, pair, 0)
    for side, at in ((0, 0), (1, ny - 8)):
        send(edges.at[side], new.at[:, :, pl.ds(at, 8), :])
        send(sat_edge.at[side], sat.at[:, pl.ds(at, 8), :])
    inside = pl.ds(8, ny - 16)
    for side, x in ((0, 0), (1, nx - 1)):
        for copy in fetch[2 * side : 2 * side + 2]:
            copy.wait()
        own = 3 * side
        for base in range(8, ny - 8, 8):

            def here(f, shift, base=base):
                return planes[f, own, base + shift : base + shift + 8, :]

            def inward(f, base=base):
                return planes[f, 1 + side, base : base + 8, :]

            def outward(f, base=base):
                ref = right if side else left
                return ref[f * ny + base : f * ny + base + 8, :]

            def put(f, value, base=base):
                if f == 5:
                    sat_out[side, base : base + 8, :] = value
                else:
                    fresh[f, side, base : base + 8, :] = value

            step_rows(here, inward if side else outward, outward if side else inward, put)
        send(fresh.at[:, side, inside, :], new.at[:, x, inside, :])
        send(sat_out.at[side, inside, :], sat.at[x, inside, :])
    for copy in waits:
        copy.wait()


def inner_planes(state):
    _, nx, ny, nz = state.shape
    return pl.pallas_call(
        inner_kernel,
        out_shape=[
            jax.ShapeDtypeStruct(state.shape, f32),
            jax.ShapeDtypeStruct((nx * ny, nz), f32),
        ],
        in_specs=[HBM],
        out_specs=[HBM, HBM],
        scratch_shapes=[
            pltpu.VMEM((5, nx, ny, nz), f32),
            pltpu.VMEM((5, nx, ny, nz), f32),
            pltpu.VMEM((nx * ny, nz), f32),
            pltpu.SemaphoreType.DMA((nx,)),
            pltpu.SemaphoreType.DMA((nx,)),
            pltpu.SemaphoreType.DMA((nx,)),
        ],
        compiler_params=pltpu.CompilerParams(vmem_limit_bytes=40 << 20),
        cost_estimate=pl.CostEstimate(flops=60_000_000, bytes_accessed=36 << 20, transcendentals=0),
        name="inner",
    )(state)


def rim_planes(state, left, right, south, north, new, sat):
    _, nx, ny, nz = state.shape
    return pl.pallas_call(
        rim_kernel,
        out_shape=[
            jax.ShapeDtypeStruct(state.shape, f32),
            jax.ShapeDtypeStruct((nx, ny, nz), f32),
        ],
        in_specs=[HBM] + [VMEM] * 4 + [HBM] * 2,
        out_specs=[HBM, HBM],
        input_output_aliases={5: 0, 6: 1},
        scratch_shapes=[
            pltpu.VMEM((5, 4, ny, nz), f32),
            pltpu.VMEM((5, 2, ny, nz), f32),
            pltpu.VMEM((2, 5, nx, 24, nz), f32),
            pltpu.VMEM((2, 5, nx, 8, nz), f32),
            pltpu.VMEM((2, ny, nz), f32),
            pltpu.VMEM((2, nx, 8, nz), f32),
            pltpu.SemaphoreType.DMA((4,)),
            pltpu.SemaphoreType.DMA((2,)),
            pltpu.SemaphoreType.DMA((8,)),
        ],
        compiler_params=pltpu.CompilerParams(vmem_limit_bytes=24 << 20),
        cost_estimate=pl.CostEstimate(flops=8_000_000, bytes_accessed=9 << 20, transcendentals=0),
        name="rim",
    )(state, left, right, south, north, new, sat.reshape(nx, ny, nz))


SUMS = 2
GROUP = 16


def grow_kernel(codes, cap, extra, *refs):
    count = len(codes)
    bufs = [refs[which] for which, _, _ in codes]
    tops = [top for _, top, _ in codes]
    slots = [slot for _, _, slot in codes]
    refs = refs[1 + max(which for which, _, _ in codes) :]
    sat_hbm, new_in = refs[:2]
    refs = refs[2 + extra :]
    radius, new, sat, near, value_out = refs[:5]
    totals = refs[5 : 5 + SUMS]
    fields, cols_v, cols_s, sat_sem, field_sem, col_sem, rad_sem, out_sem = refs[5 + SUMS :]
    nx, ny = new.shape[1], new.shape[2]
    get_sat = pltpu.make_async_copy(sat_hbm, sat, sat_sem)
    get_sat.start()
    for i in range(count):
        at = tops[i] + 3 * cap
        cols_v[i : i + 1, :] = bufs[i][at : at + 1, :].astype(i32)
    get_cols = pltpu.make_async_copy(cols_v, cols_s, col_sem)
    get_cols.start()
    get_fields = pltpu.make_async_copy(new_in.at[pl.ds(3, 2)], fields, field_sem)
    get_fields.start()
    for total in totals:
        total[...] = jnp.zeros_like(total)
    get_cols.wait()
    get_sat.wait()
    put_radius = []
    for i in range(count):

        def gather(step, carry, i=i):
            for u in range(GROUP):
                j = step * GROUP + u
                near[pl.ds(i * cap + j, 1), :] = sat[pl.ds(cols_s[i, j], 1), :]
            return carry

        lax.fori_loop(0, cap // GROUP, gather, 0)
    for i in range(count):
        ref, top = bufs[i], tops[i]
        for at in range(0, cap, 8):
            rad = ref[top + at : top + at + 8, :]
            sol = ref[top + cap + at : top + cap + at + 8, :]
            mul = ref[top + 2 * cap + at : top + 2 * cap + at + 8, :]
            rows = slice(i * cap + at, i * cap + at + 8)
            alive = mul > 0.0
            start = jnp.where(alive, rad, 1.0)
            square = start * start
            base = square + growth_coef * near[rows, :]
            sol = (growth_coef * solute_coef) * sol
            inv = 1.0 / start
            for _ in range(ITERS):
                inside = base + inv * (sol * (inv * inv) - growth_coef * curvature_coef)
                inside = jnp.maximum(inside, floor_square)
                inv = lax.rsqrt(inside)
            value = inside * inv
            value_out[rows, :] = jnp.where(alive, value, 0.0)
            near[rows, :] = mul * (value * inside - start * square)
        copy = pltpu.make_async_copy(
            value_out.at[pl.ds(i * cap, cap), :],
            radius.at[pl.ds(slots[i] * cap, cap), :],
            rad_sem.at[i],
        )
        copy.start()
        put_radius.append(copy)

    def scatter(step, carry):
        for u in range(4):
            j = step * 4 + u
            for i in range(count):
                c = cols_s[i, j]
                totals[i % SUMS][pl.ds(c, 1), :] += near[pl.ds(i * cap + j, 1), :]
        return carry

    lax.fori_loop(0, cap // 4, scatter, 0)
    get_fields.wait()

    def put(x):
        return pltpu.make_async_copy(fields.at[:, x], new.at[pl.ds(3, 2), x], out_sem.at[x])

    def final(x, carry):
        def rows(step, inner):
            at = step * 32
            tot = totals[0][pl.ds(x * ny + at, 32), :]
            for total in totals[1:]:
                tot = tot + total[pl.ds(x * ny + at, 32), :]
            fields[0, x, pl.ds(at, 32), :] += latent_coef * tot
            fields[1, x, pl.ds(at, 32), :] -= condense_coef * tot
            return inner

        lax.fori_loop(0, ny // 32, rows, 0)
        put(x).start()
        return carry

    lax.fori_loop(0, nx, final, 0)
    for copy in put_radius:
        copy.wait()
    for x in range(nx):
        put(x).wait()


def grow_blocks(bufs, codes, cap, sat, new, radius=()):
    extra = len(radius)
    _, nx, ny, nz = new.shape
    n = len(bufs)
    count = len(codes)
    return pl.pallas_call(
        functools.partial(grow_kernel, codes, cap, extra),
        out_shape=[
            jax.ShapeDtypeStruct((CODES * cap, nz), f32),
            jax.ShapeDtypeStruct(new.shape, f32),
        ],
        in_specs=[VMEM] * n + [HBM] * (2 + extra),
        out_specs=[HBM, HBM],
        input_output_aliases={n + 1: 1} | {n + 2: 0 for _ in radius},
        scratch_shapes=[
            pltpu.VMEM((nx * ny, nz), f32),
            pltpu.VMEM((count * cap, nz), f32),
            pltpu.VMEM((count * cap, nz), f32),
        ]
        + [pltpu.VMEM((nx * ny, nz), f32) for _ in range(SUMS)]
        + [
            pltpu.VMEM((2, nx, ny, nz), f32),
            pltpu.VMEM((8, 128), i32),
            pltpu.SMEM((8, 128), i32),
            pltpu.SemaphoreType.DMA,
            pltpu.SemaphoreType.DMA,
            pltpu.SemaphoreType.DMA,
            pltpu.SemaphoreType.DMA((count,)),
            pltpu.SemaphoreType.DMA((nx,)),
        ],
        compiler_params=pltpu.CompilerParams(vmem_limit_bytes=32 << 20),
        cost_estimate=pl.CostEstimate(flops=20_000_000, bytes_accessed=16 << 20, transcendentals=0),
        name="grow",
    )(*bufs, sat, new, *radius)


def moved(value, dx, dy):
    nx, ny = lax.axis_size("gx"), lax.axis_size("gy")
    pairs = [
        (tx * ny + ty, (tx + dx) % nx * ny + (ty + dy) % ny) for tx in range(nx) for ty in range(ny)
    ]
    return lax.ppermute(value, ("gx", "gy"), pairs)


def on_device(state, radius, solute, multiplicity, block_column, destination, live_blocks):
    _, nx, ny, nz = state.shape
    cap = radius.shape[0] // 8
    one = parcel_rows(cap)
    *sides, own = pack_blocks(
        radius, solute, multiplicity, block_column, destination, live_blocks, state
    )
    first = [moved(side, dx, dy) for side, (dx, dy, _, _) in zip(sides, FIRST)]
    new, sat = inner_planes(state)
    first, new, sat = lax.optimization_barrier((first, new, sat))
    tops = (5 * ny, 5 * ny, 5 * nx, 5 * nx)
    second = [
        moved(side[top + one : top + 2 * one], dx, dy)
        for side, top, (dx, dy, _) in zip(first, tops, SECOND)
    ]
    from_right, from_left, from_north, from_south = first
    new, sat = rim_planes(state, from_left, from_right, from_south, from_north, new, sat)
    sat = sat.reshape(nx * ny, nz)
    codes = ((0, 0, OWN),) + tuple(
        (1 + i, top, end) for i, (top, (_, _, end, _)) in enumerate(zip(tops, FIRST))
    )
    value, new = grow_blocks([own] + first, codes, cap, sat, new)
    codes = tuple((i, 0, code) for i, (_, _, code) in enumerate(SECOND))
    value, new = grow_blocks(second, codes, cap, sat, new, (value,))
    return new, value


def solution(mesh):
    placed = (
        P(None, "gx", "gy", None),
        P(("gx", "gy"), None),
        P(("gx", "gy"), None),
        P(("gx", "gy"), None),
        P(("gx", "gy")),
        P(("gx", "gy"), None),
        P(("gx", "gy")),
    )
    return jax.shard_map(
        on_device,
        mesh=mesh,
        in_specs=placed,
        out_specs=(P(None, "gx", "gy", None), P(("gx", "gy"), None)),
        check_vma=False,
    )
```

```python
import functools

import jax
import jax.numpy as jnp
from jax import lax
from jax.experimental import pallas as pl
from jax.experimental.pallas import tpu as pltpu
from jax.sharding import PartitionSpec as P

ITERS = 4
CODES = 9
OWN = 4

smag_coef = 0.02
buoyancy_coef = 0.5
growth_coef = 0.6
curvature_coef = 0.1
solute_coef = 0.3
floor_square = 0.04
condense_coef = 0.5
latent_coef = 0.8
epsilon = 1e-06

f32 = jnp.float32
bf16 = jnp.bfloat16
i32 = jnp.int32
HBM = pl.BlockSpec(memory_space=pltpu.HBM)
VMEM = pl.BlockSpec(memory_space=pltpu.VMEM)
SMEM = pl.BlockSpec(memory_space=pltpu.SMEM)


def in_hbm(*values):
    return [pltpu.with_memory_space_constraint(value, pltpu.HBM) for value in values]


def iota(shape, dim):
    return lax.broadcasted_iota(i32, shape, dim)


def halves(value):
    high = value.astype(bf16)
    low = (value - high.astype(f32)).astype(bf16)
    return high, low


FIRST = ((-1, 0, 1, 0), (1, 0, 7, 8), (0, -1, 3, 6), (0, 1, 5, 2))
SECOND = ((0, -1, 0), (0, 1, 8), (1, 0, 6), (-1, 0, 2))


def parcel_rows(cap):
    return 3 * cap + 8


def pack_kernel(
    cap, live_ref, code_hbm, col_hbm, rad_hbm, sol_hbm, mul_hbm, state,
    west_out, east_out, south_out, north_out, own_out,
    code_ref, col_ref, drops, edges, onehot, values, sems,
):
    nx, ny = state.shape[1], state.shape[2]
    tops = (5 * ny, 5 * ny, 5 * nx, 5 * nx)
    sides = (west_out, east_out, south_out, north_out)
    small = [
        pltpu.make_async_copy(code_hbm, code_ref, sems.at[0]),
        pltpu.make_async_copy(col_hbm, col_ref, sems.at[1]),
    ]
    big = [
        pltpu.make_async_copy(ref, drops.at[part], sems.at[2 + part])
        for part, ref in enumerate((rad_hbm, sol_hbm, mul_hbm))
    ]
    edge = [
        pltpu.make_async_copy(state.at[:, :, pl.ds(0, 8), :], edges.at[0], sems.at[5]),
        pltpu.make_async_copy(state.at[:, :, pl.ds(ny - 8, 8), :], edges.at[1], sems.at[6]),
    ]
    rims = [
        pltpu.make_async_copy(
            state.at[f, x], side.at[pl.ds(f * ny, ny), :], sems.at[7 + 5 * which + f]
        )
        for which, (side, x) in enumerate(((west_out, 0), (east_out, nx - 1)))
        for f in range(5)
    ]
    for copy in small + big + edge + rims:
        copy.start()
    for copy in small:
        copy.wait()
    rows, lanes = code_ref.shape
    code = code_ref[...]
    live = iota((rows, lanes), 0) * lanes + iota((rows, lanes), 1) < live_ref[0]
    hits = [jnp.where((code == k) & live, 1.0, 0.0) for k in range(CODES)]
    hit = jnp.concatenate(hits, axis=0)
    wide = iota((lanes, 2 * lanes), 1)
    before = jnp.where((iota((lanes, 2 * lanes), 0) < wide) | (wide >= lanes), 1.0, 0.0)
    inside = jnp.dot(hit, before, preferred_element_type=f32)
    high = CODES * rows
    a, b = iota((high, high), 0), iota((high, high), 1)
    above = jnp.where((a // rows == b // rows) & (b < a), 1.0, 0.0)
    rank = inside[:, :lanes] + jnp.dot(above, inside[:, lanes:], preferred_element_type=f32)
    place = jnp.where(hit > 0.0, rank, -1.0).astype(i32)
    slot = iota((cap, lanes), 0)
    for k in range(CODES):
        for row in range(rows):
            spot = place[k * rows + row : k * rows + row + 1, :]
            onehot[k * cap : (k + 1) * cap, row * lanes : (row + 1) * lanes] = jnp.where(
                slot == spot, 1.0, 0.0
            ).astype(bf16)
    for part in range(3):
        big[part].wait()
        top, low = halves(drops[part])
        values[:, part * 128 : part * 128 + 128] = top
        values[:, 384 + part * 128 : 512 + part * 128] = low
    moved = jnp.dot(onehot[...], values[...], preferred_element_type=f32)
    moved = moved[:, :384] + moved[:, 384:]
    col = col_ref[...]
    coarse = (col // 16 * 16).astype(f32)
    fine = (col % 16).astype(f32)
    flat = jnp.concatenate(
        [
            jnp.concatenate([item[row : row + 1] for row in range(rows)], axis=1)
            for item in (coarse, fine)
        ]
        + [jnp.zeros((6, rows * lanes), f32)],
        axis=0,
    ).astype(bf16)
    spots = {OWN: (own_out, 0)}
    for side, top, (_, _, end, diagonal) in zip(sides, tops, FIRST):
        spots[end] = (side, top)
        spots[diagonal] = (side, top + parcel_rows(cap))
    for k in range(CODES):
        ref, at = spots[k]
        for part in range(3):
            ref[at + part * cap : at + (part + 1) * cap, :] = moved[
                k * cap : (k + 1) * cap, part * 128 : (part + 1) * 128
            ]
        cols = lax.dot_general(
            flat,
            onehot[k * cap : (k + 1) * cap, :],
            (((1,), (1,)), ((), ())),
            preferred_element_type=f32,
        )
        ref[at + 3 * cap : at + 3 * cap + 8, :] = jnp.broadcast_to(cols[0:1] + cols[1:2], (8, 128))
    for copy in edge:
        copy.wait()
    for f in range(5):
        for x in range(nx):
            at = f * nx + x
            south_out[at : at + 1, :] = edges[0, f, x, 0:1, :]
            north_out[at : at + 1, :] = edges[1, f, x, 7:8, :]
    for copy in rims:
        copy.wait()


def pack_blocks(rad, sol, mul, col, code, count, state):
    blocks = rad.shape[0]
    cap = blocks // 8
    rows = blocks // 128
    _, nx, ny, nz = state.shape
    one = parcel_rows(cap)
    heights = [5 * ny + 2 * one] * 2 + [5 * nx + 2 * one] * 2 + [one]
    return pl.pallas_call(
        functools.partial(pack_kernel, cap),
        out_shape=[pltpu.VMEM((height, nz), f32) for height in heights],
        in_specs=[SMEM] + [HBM] * 6,
        out_specs=[VMEM] * 5,
        scratch_shapes=[
            pltpu.VMEM((rows, 128), i32),
            pltpu.VMEM((rows, 128), i32),
            pltpu.VMEM((3, blocks, nz), f32),
            pltpu.VMEM((2, 5, nx, 8, nz), f32),
            pltpu.VMEM((CODES * cap, blocks), bf16),
            pltpu.VMEM((blocks, 6 * nz), bf16),
            pltpu.SemaphoreType.DMA((17,)),
        ],
        compiler_params=pltpu.CompilerParams(vmem_limit_bytes=40 << 20),
        cost_estimate=pl.CostEstimate(flops=2_000_000_000, bytes_accessed=4 << 20, transcendentals=0),
        name="pack",
    )(count, *in_hbm(code.reshape(rows, 128), col.reshape(rows, 128), rad, sol, mul, state))


def step_rows(here, west, east, put):
    lane = iota((8, 128), 1)

    def around(f):
        c = here(f, 0)
        up = jnp.where(lane == 127, c, pltpu.roll(c, 127, 1))
        low = jnp.where(lane == 0, c, pltpu.roll(c, 1, 1))
        return c, east(f), west(f), here(f, 1), here(f, -1), up, low

    def lap(parts):
        c, e, w, n, s, up, low = parts
        return e + w + n + s + up + low - 6.0 * c

    def slopes(parts):
        c, e, w, n, s, up, low = parts
        return e - w, n - s, up - low

    pu, pv, pw = around(0), around(1), around(2)
    du, dv, dw = slopes(pu), slopes(pv), slopes(pw)
    strain = 2.0 * (du[0] * du[0] + dv[1] * dv[1] + dw[2] * dw[2])
    uv = du[1] + dv[0]
    uw = du[2] + dw[0]
    vw = dv[2] + dw[1]
    strain = strain + uv * uv + uw * uw + vw * vw
    visc = smag_coef * jnp.sqrt(0.25 * strain + epsilon)
    put(0, pu[0] + visc * lap(pu))
    put(1, pv[0] + visc * lap(pv))
    pb = around(3)
    put(2, pw[0] + visc * lap(pw) + buoyancy_coef * pb[0])
    fb = pb[0] + visc * lap(pb)
    put(3, fb)
    pq = around(4)
    fq = pq[0] + visc * lap(pq)
    put(4, fq)
    put(5, fq - 0.5 * fb)


def inner_kernel(state, new, buoy, vapour, sat, planes, fresh, in_sem, out_sem):
    nx, ny = state.shape[1], state.shape[2]
    inside = pl.ds(8, ny - 16)
    last = (buoy, vapour, sat)

    def fetch(x):
        return pltpu.make_async_copy(state.at[:, x], planes.at[:, x], in_sem.at[x])

    def store(x):
        return pltpu.make_async_copy(
            fresh.at[:, x, inside, :], new.at[pl.ds(0, 3), x, inside, :], out_sem.at[x]
        )

    for x in range(nx):
        fetch(x).start()
    fetch(0).wait()
    fetch(1).wait()

    def body(x, carry):
        fetch(x + 1).wait()
        for base in range(8, ny - 8, 8):

            def here(f, shift, base=base):
                return planes[f, x, base + shift : base + shift + 8, :]

            def west(f, base=base):
                return planes[f, x - 1, base : base + 8, :]

            def east(f, base=base):
                return planes[f, x + 1, base : base + 8, :]

            def put(f, value, base=base):
                if f >= 3:
                    last[f - 3][x, base : base + 8, :] = value
                else:
                    fresh[f, x, base : base + 8, :] = value

            step_rows(here, west, east, put)
        store(x).start()
        return carry

    lax.fori_loop(1, nx - 1, body, 0)
    for x in range(1, nx - 1):
        store(x).wait()


def edge_rows(planes, x, side, halo, west, east, put):
    ny = planes.shape[2]
    at = side * (ny - 8)
    sub = iota((8, 128), 0)

    def here(f, shift):
        if shift == 2 * side - 1:
            c = planes[f, x, at : at + 8, :]
            if side:
                return jnp.where(sub == 7, halo(f), pltpu.roll(c, 7, 0))
            return jnp.where(sub == 0, halo(f), pltpu.roll(c, 1, 0))
        return planes[f, x, at + shift : at + shift + 8, :]

    step_rows(here, lambda f: west(f, at), lambda f: east(f, at), put)


def ends_kernel(planes, south, north, new_in, b_in, q_in, s_in, new, buoy, vapour, sat, edges, out_sem):
    nx, ny = planes.shape[1], planes.shape[2]
    last = (buoy, vapour, sat)

    def step(x, carry):
        for side, ref in ((0, south), (1, north)):

            def put(f, value, side=side):
                if f >= 3:
                    last[f - 3][x, side * (ny - 8) : side * (ny - 8) + 8, :] = value
                else:
                    edges[side, f, x] = value

            edge_rows(
                planes,
                x,
                side,
                lambda f, ref=ref: ref[pl.ds(f * nx + x, 1), :],
                lambda f, at: planes[f, x - 1, at : at + 8, :],
                lambda f, at: planes[f, x + 1, at : at + 8, :],
                put,
            )
        return carry

    lax.fori_loop(1, nx - 1, step, 0, unroll=2)
    copies = [
        pltpu.make_async_copy(
            edges.at[side, :, pl.ds(1, nx - 2)],
            new.at[pl.ds(0, 3), pl.ds(1, nx - 2), pl.ds(side * (ny - 8), 8), :],
            out_sem.at[side],
        )
        for side in range(2)
    ]
    for copy in copies:
        copy.start()
    for copy in copies:
        copy.wait()


def rim_kernel(
    planes, left, right, south, north, new_in, b_in, q_in, s_in, new, buoy, vapour, sat, fresh, out_sem
):
    nx, ny = planes.shape[1], planes.shape[2]
    last = (buoy, vapour, sat)
    copies = []
    for side, x in ((0, 0), (1, nx - 1)):

        def inward(f, at, x=x, side=side):
            return planes[f, x + 1 - 2 * side, at : at + 8, :]

        def outward(f, at, side=side):
            ref = right if side else left
            return ref[f * ny + at : f * ny + at + 8, :]

        west, east = (inward, outward) if side else (outward, inward)
        for at in range(0, ny, 8):

            def put(f, value, at=at, x=x, side=side):
                if f >= 3:
                    last[f - 3][x, at : at + 8, :] = value
                else:
                    fresh[f, side, at : at + 8, :] = value

            if at in (0, ny - 8):
                ref = north if at else south
                edge_rows(
                    planes,
                    x,
                    1 if at else 0,
                    lambda f, ref=ref, x=x: ref[f * nx + x : f * nx + x + 1, :],
                    west,
                    east,
                    put,
                )
            else:
                step_rows(
                    lambda f, shift, x=x, at=at: planes[f, x, at + shift : at + shift + 8, :],
                    lambda f, at=at: west(f, at),
                    lambda f, at=at: east(f, at),
                    put,
                )
        copy = pltpu.make_async_copy(
            fresh.at[:, side], new.at[pl.ds(0, 3), x], out_sem.at[side]
        )
        copy.start()
        copies.append(copy)
    for copy in copies:
        copy.wait()


def inner_planes(state):
    _, nx, ny, nz = state.shape
    return pl.pallas_call(
        inner_kernel,
        out_shape=[pltpu.HBM(state.shape, f32)]
        + [pltpu.VMEM((nx, ny, nz), f32)] * 3
        + [pltpu.VMEM(state.shape, f32)],
        in_specs=[HBM],
        out_specs=[HBM] + [VMEM] * 4,
        scratch_shapes=[
            pltpu.VMEM((3, nx, ny, nz), f32),
            pltpu.SemaphoreType.DMA((nx,)),
            pltpu.SemaphoreType.DMA((nx,)),
        ],
        compiler_params=pltpu.CompilerParams(vmem_limit_bytes=16 << 20),
        cost_estimate=pl.CostEstimate(flops=60_000_000, bytes_accessed=36 << 20, transcendentals=0),
        name="inner",
    )(*in_hbm(state))


def edge_planes(kernel, planes, halos, fields, scratch, name):
    new, buoy = fields[:2]
    at = 1 + len(halos)
    return pl.pallas_call(
        kernel,
        out_shape=[pltpu.HBM(new.shape, f32)] + [pltpu.VMEM(buoy.shape, f32)] * 3,
        in_specs=[VMEM] * at + [HBM] + [VMEM] * 3,
        out_specs=[HBM] + [VMEM] * 3,
        input_output_aliases={at + i: i for i in range(4)},
        scratch_shapes=[scratch, pltpu.SemaphoreType.DMA((2,))],
        compiler_params=pltpu.CompilerParams(vmem_limit_bytes=8 << 20),
        cost_estimate=pl.CostEstimate(flops=8_000_000, bytes_accessed=9 << 20, transcendentals=0),
        name=name,
    )(planes, *halos, *fields)


SUMS = 3
GROUP = 8


def grow_codes(codes, cap, bufs, sat, totals, radius, near, mass, value_out, cols_v, cols_s, col_sem, rad_sem):
    count = len(codes)
    for i, (which, top, _) in enumerate(codes):
        at = top + 3 * cap
        cols_v[i : i + 1, :] = bufs[which][at : at + 1, :].astype(i32)
    get_cols = pltpu.make_async_copy(cols_v, cols_s, col_sem)
    get_cols.start()
    yield
    get_cols.wait()
    put_radius = []
    for i in range(count + 1):

        def rows(step, carry, i=i):
            for u in range(GROUP):
                j = step * GROUP + u
                if i < count:
                    near[i % 2][pl.ds(j, 1), :] = sat[pl.ds(cols_s[i, j], 1), :]
                if i > 0:
                    totals[u % SUMS][pl.ds(cols_s[i - 1, j], 1), :] += mass[(i - 1) % 2][pl.ds(j, 1), :]
            return carry

        lax.fori_loop(0, cap // GROUP, rows, 0)
        if i == count:
            break
        which, top, slot = codes[i]
        ref = bufs[which]
        for at in range(0, cap, 8):
            rad = ref[top + at : top + at + 8, :]
            sol = ref[top + cap + at : top + cap + at + 8, :]
            mul = ref[top + 2 * cap + at : top + 2 * cap + at + 8, :]
            alive = mul > 0.0
            start = jnp.where(alive, rad, 1.0)
            square = start * start
            base = square + growth_coef * near[i % 2][at : at + 8, :]
            sol = (growth_coef * solute_coef) * sol
            inv = 1.0 / start
            for _ in range(ITERS):
                inside = base + inv * (sol * (inv * inv) - growth_coef * curvature_coef)
                inside = jnp.maximum(inside, floor_square)
                inv = lax.rsqrt(inside)
            value = inside * inv
            value_out[i * cap + at : i * cap + at + 8, :] = jnp.where(alive, value, 0.0)
            mass[i % 2][at : at + 8, :] = mul * (value * inside - start * square)
        copy = pltpu.make_async_copy(
            value_out.at[pl.ds(i * cap, cap), :],
            radius.at[pl.ds(slot * cap, cap), :],
            rad_sem.at[i],
        )
        copy.start()
        put_radius.append(copy)
    yield
    for copy in put_radius:
        copy.wait()


def early_kernel(codes, cap, n, *refs):
    bufs, sat = refs[:n], refs[n]
    radius = refs[n + 1]
    totals = refs[n + 2 : n + 2 + SUMS]
    near0, near1, mass0, mass1, *rest = refs[n + 2 + SUMS :]
    steps = grow_codes(codes, cap, bufs, sat, totals, radius, (near0, near1), (mass0, mass1), *rest)
    next(steps)
    for total in totals:
        total[...] = jnp.zeros_like(total)
    for _ in steps:
        pass


def late_kernel(codes, cap, n, *refs):
    bufs, sat, buoy, vapour = refs[:n], refs[n], refs[n + 1], refs[n + 2]
    refs = refs[n + 3 + SUMS + 2 :]
    radius, new = refs[:2]
    totals = refs[2 : 2 + SUMS]
    near0, near1, mass0, mass1, *rest, fields, out_sem = refs[2 + SUMS :]
    nx, ny = new.shape[1], new.shape[2]
    steps = grow_codes(codes, cap, bufs, sat, totals, radius, (near0, near1), (mass0, mass1), *rest)
    next(steps)
    next(steps)

    def put(x):
        return pltpu.make_async_copy(fields.at[:, x], new.at[pl.ds(3, 2), x], out_sem.at[x])

    def final(x, carry):
        for at in range(0, ny, 8):
            tot = totals[0][pl.ds(x * ny + at, 8), :]
            for total in totals[1:]:
                tot = tot + total[pl.ds(x * ny + at, 8), :]
            fields[0, x, at : at + 8, :] = buoy[x, at : at + 8, :] + latent_coef * tot
            fields[1, x, at : at + 8, :] = vapour[x, at : at + 8, :] - condense_coef * tot
        put(x).start()
        return carry

    lax.fori_loop(0, nx, final, 0)
    for _ in steps:
        pass
    for x in range(nx):
        put(x).wait()


def grow_scratch(count, cap, nz):
    return [pltpu.VMEM((cap, nz), f32)] * 4 + [
        pltpu.VMEM((count * cap, nz), f32),
        pltpu.VMEM((8, 128), i32),
        pltpu.SMEM((8, 128), i32),
        pltpu.SemaphoreType.DMA,
        pltpu.SemaphoreType.DMA((count,)),
    ]


def grow_early(bufs, codes, cap, sat):
    cells, nz = sat.shape
    n, count = len(bufs), len(codes)
    return pl.pallas_call(
        functools.partial(early_kernel, codes, cap, n),
        out_shape=[pltpu.HBM((CODES * cap, nz), f32)] + [pltpu.VMEM((cells, nz), f32)] * SUMS,
        in_specs=[VMEM] * (n + 1),
        out_specs=[HBM] + [VMEM] * SUMS,
        scratch_shapes=grow_scratch(count, cap, nz),
        compiler_params=pltpu.CompilerParams(vmem_limit_bytes=8 << 20),
        cost_estimate=pl.CostEstimate(flops=20_000_000, bytes_accessed=16 << 20, transcendentals=0),
        name="early",
    )(*bufs, sat)


def grow_late(bufs, codes, cap, sat, buoy, vapour, totals, new, radius):
    cells, nz = sat.shape
    _, nx, ny, _ = new.shape
    n, count = len(bufs), len(codes)
    at = n + 3
    return pl.pallas_call(
        functools.partial(late_kernel, codes, cap, n),
        out_shape=[pltpu.HBM(radius.shape, f32), pltpu.HBM(new.shape, f32)]
        + [pltpu.VMEM((cells, nz), f32)] * SUMS,
        in_specs=[VMEM] * (at + SUMS) + [HBM] * 2,
        out_specs=[HBM] * 2 + [VMEM] * SUMS,
        input_output_aliases={at + i: 2 + i for i in range(SUMS)}
        | {at + SUMS: 1, at + SUMS + 1: 0},
        scratch_shapes=grow_scratch(count, cap, nz)
        + [pltpu.VMEM((2, nx, ny, nz), f32), pltpu.SemaphoreType.DMA((nx,))],
        compiler_params=pltpu.CompilerParams(vmem_limit_bytes=12 << 20),
        cost_estimate=pl.CostEstimate(flops=20_000_000, bytes_accessed=16 << 20, transcendentals=0),
        name="late",
    )(*bufs, sat, buoy, vapour, *totals, new, radius)[:2]


def moved(value, dx, dy):
    nx, ny = lax.axis_size("gx"), lax.axis_size("gy")
    pairs = [
        (tx * ny + ty, (tx + dx) % nx * ny + (ty + dy) % ny) for tx in range(nx) for ty in range(ny)
    ]
    return lax.ppermute(value, ("gx", "gy"), pairs)


def on_device(state, radius, solute, multiplicity, block_column, destination, live_blocks):
    _, nx, ny, nz = state.shape
    cap = radius.shape[0] // 8
    one = parcel_rows(cap)
    *sides, own = pack_blocks(
        radius, solute, multiplicity, block_column, destination, live_blocks, state
    )
    first = [moved(side, dx, dy) for side, (dx, dy, _, _) in zip(sides, FIRST)]
    *fields, planes = inner_planes(state)
    along_x, along_y = first[:2], first[2:]
    along_y, fields, planes = lax.optimization_barrier((along_y, fields, planes))
    from_north, from_south = along_y
    scratch = pltpu.VMEM((2, 3, nx, 8, nz), f32)
    fields = edge_planes(ends_kernel, planes, [from_south, from_north], fields, scratch, "ends")
    along_x, fields = lax.optimization_barrier((along_x, fields))
    first = [*along_x, *along_y]
    from_right, from_left = along_x
    tops = (5 * ny, 5 * ny, 5 * nx, 5 * nx)
    second = [
        moved(side[top + one : top + 2 * one], dx, dy)
        for side, top, (dx, dy, _) in zip(first, tops, SECOND)
    ]
    scratch = pltpu.VMEM((3, 2, ny, nz), f32)
    halos = [from_left, from_right, from_south, from_north]
    new, buoy, vapour, sat = edge_planes(rim_kernel, planes, halos, fields, scratch, "rim")
    sat = sat.reshape(nx * ny, nz)
    codes = ((0, 0, OWN),) + tuple(
        (1 + i, top, end) for i, (top, (_, _, end, _)) in enumerate(zip(tops, FIRST))
    )
    value, *totals = grow_early([own] + first, codes, cap, sat)
    codes = tuple((i, 0, code) for i, (_, _, code) in enumerate(SECOND))
    value, new = grow_late(second, codes, cap, sat, buoy, vapour, totals, new, value)
    return new, value


def solution(mesh):
    placed = (
        P(None, "gx", "gy", None),
        P(("gx", "gy"), None),
        P(("gx", "gy"), None),
        P(("gx", "gy"), None),
        P(("gx", "gy")),
        P(("gx", "gy"), None),
        P(("gx", "gy")),
    )
    return jax.shard_map(
        on_device,
        mesh=mesh,
        in_specs=placed,
        out_specs=(P(None, "gx", "gy", None), P(("gx", "gy"), None)),
        check_vma=False,
    )
```

```python
import functools

import jax
import jax.numpy as jnp
from jax import lax
from jax.experimental import pallas as pl
from jax.experimental.pallas import tpu as pltpu
from jax.sharding import PartitionSpec as P

ITERS = 4
CODES = 9
OWN = 4

smag_coef = 0.02
buoyancy_coef = 0.5
growth_coef = 0.6
curvature_coef = 0.1
solute_coef = 0.3
floor_square = 0.04
condense_coef = 0.5
latent_coef = 0.8
epsilon = 1e-06

f32 = jnp.float32
bf16 = jnp.bfloat16
i32 = jnp.int32
HBM = pl.BlockSpec(memory_space=pltpu.HBM)
VMEM = pl.BlockSpec(memory_space=pltpu.VMEM)
SMEM = pl.BlockSpec(memory_space=pltpu.SMEM)


def in_hbm(*values):
    return [pltpu.with_memory_space_constraint(value, pltpu.HBM) for value in values]


def iota(shape, dim):
    return lax.broadcasted_iota(i32, shape, dim)


def halves(value):
    high = value.astype(bf16)
    low = (value - high.astype(f32)).astype(bf16)
    return high, low


FIRST = ((-1, 0, 1, 0), (1, 0, 7, 8), (0, -1, 3, 6), (0, 1, 5, 2))
SECOND = ((0, -1, 0), (0, 1, 8), (1, 0, 6), (-1, 0, 2))


def parcel_rows(cap):
    return 3 * cap + 8


def pack_kernel(
    cap, live_ref, code_hbm, col_hbm, rad_hbm, sol_hbm, mul_hbm, state,
    west_out, east_out, south_out, north_out, own_out,
    code_ref, col_ref, drops, edges, onehot, values, sems,
):
    nx, ny = state.shape[1], state.shape[2]
    tops = (5 * ny, 5 * ny, 5 * nx, 5 * nx)
    sides = (west_out, east_out, south_out, north_out)
    small = [
        pltpu.make_async_copy(code_hbm, code_ref, sems.at[0]),
        pltpu.make_async_copy(col_hbm, col_ref, sems.at[1]),
    ]
    big = [
        pltpu.make_async_copy(ref, drops.at[part], sems.at[2 + part])
        for part, ref in enumerate((rad_hbm, sol_hbm, mul_hbm))
    ]
    edge = [
        pltpu.make_async_copy(state.at[:, :, pl.ds(0, 8), :], edges.at[0], sems.at[5]),
        pltpu.make_async_copy(state.at[:, :, pl.ds(ny - 8, 8), :], edges.at[1], sems.at[6]),
    ]
    rims = [
        pltpu.make_async_copy(
            state.at[f, x], side.at[pl.ds(f * ny, ny), :], sems.at[7 + 5 * which + f]
        )
        for which, (side, x) in enumerate(((west_out, 0), (east_out, nx - 1)))
        for f in range(5)
    ]
    for copy in small + big + edge + rims:
        copy.start()
    for copy in small:
        copy.wait()
    rows, lanes = code_ref.shape
    code = code_ref[...]
    live = iota((rows, lanes), 0) * lanes + iota((rows, lanes), 1) < live_ref[0]
    hits = [jnp.where((code == k) & live, 1.0, 0.0) for k in range(CODES)]
    hit = jnp.concatenate(hits, axis=0)
    wide = iota((lanes, 2 * lanes), 1)
    before = jnp.where((iota((lanes, 2 * lanes), 0) < wide) | (wide >= lanes), 1.0, 0.0)
    inside = jnp.dot(hit, before, preferred_element_type=f32)
    high = CODES * rows
    a, b = iota((high, high), 0), iota((high, high), 1)
    above = jnp.where((a // rows == b // rows) & (b < a), 1.0, 0.0)
    rank = inside[:, :lanes] + jnp.dot(above, inside[:, lanes:], preferred_element_type=f32)
    place = jnp.where(hit > 0.0, rank, -1.0).astype(i32)
    slot = iota((cap, lanes), 0)
    for k in range(CODES):
        for row in range(rows):
            spot = place[k * rows + row : k * rows + row + 1, :]
            onehot[k * cap : (k + 1) * cap, row * lanes : (row + 1) * lanes] = jnp.where(
                slot == spot, 1.0, 0.0
            ).astype(bf16)
    for part in range(3):
        big[part].wait()
        top, low = halves(drops[part])
        values[:, part * 128 : part * 128 + 128] = top
        values[:, 384 + part * 128 : 512 + part * 128] = low
    moved = jnp.dot(onehot[...], values[...], preferred_element_type=f32)
    moved = moved[:, :384] + moved[:, 384:]
    col = col_ref[...]
    coarse = (col // 16 * 16).astype(f32)
    fine = (col % 16).astype(f32)
    flat = jnp.concatenate(
        [
            jnp.concatenate([item[row : row + 1] for row in range(rows)], axis=1)
            for item in (coarse, fine)
        ]
        + [jnp.zeros((6, rows * lanes), f32)],
        axis=0,
    ).astype(bf16)
    spots = {OWN: (own_out, 0)}
    for side, top, (_, _, end, diagonal) in zip(sides, tops, FIRST):
        spots[end] = (side, top)
        spots[diagonal] = (side, top + parcel_rows(cap))
    for k in range(CODES):
        ref, at = spots[k]
        for part in range(3):
            ref[at + part * cap : at + (part + 1) * cap, :] = moved[
                k * cap : (k + 1) * cap, part * 128 : (part + 1) * 128
            ]
        cols = lax.dot_general(
            flat,
            onehot[k * cap : (k + 1) * cap, :],
            (((1,), (1,)), ((), ())),
            preferred_element_type=f32,
        )
        ref[at + 3 * cap : at + 3 * cap + 8, :] = jnp.broadcast_to(cols[0:1] + cols[1:2], (8, 128))
    for copy in edge:
        copy.wait()
    for f in range(5):
        for x in range(nx):
            at = f * nx + x
            south_out[at : at + 1, :] = edges[0, f, x, 0:1, :]
            north_out[at : at + 1, :] = edges[1, f, x, 7:8, :]
    for copy in rims:
        copy.wait()


def pack_blocks(rad, sol, mul, col, code, count, state):
    blocks = rad.shape[0]
    cap = blocks // 8
    rows = blocks // 128
    _, nx, ny, nz = state.shape
    one = parcel_rows(cap)
    heights = [5 * ny + 2 * one] * 2 + [5 * nx + 2 * one] * 2 + [one]
    return pl.pallas_call(
        functools.partial(pack_kernel, cap),
        out_shape=[pltpu.VMEM((height, nz), f32) for height in heights],
        in_specs=[SMEM] + [HBM] * 6,
        out_specs=[VMEM] * 5,
        scratch_shapes=[
            pltpu.VMEM((rows, 128), i32),
            pltpu.VMEM((rows, 128), i32),
            pltpu.VMEM((3, blocks, nz), f32),
            pltpu.VMEM((2, 5, nx, 8, nz), f32),
            pltpu.VMEM((CODES * cap, blocks), bf16),
            pltpu.VMEM((blocks, 6 * nz), bf16),
            pltpu.SemaphoreType.DMA((17,)),
        ],
        compiler_params=pltpu.CompilerParams(vmem_limit_bytes=40 << 20),
        cost_estimate=pl.CostEstimate(flops=2_000_000_000, bytes_accessed=4 << 20, transcendentals=0),
        name="pack",
    )(count, *in_hbm(code.reshape(rows, 128), col.reshape(rows, 128), rad, sol, mul, state))


def step_rows(here, west, east, put):
    lane = iota((8, 128), 1)

    def around(f):
        c = here(f, 0)
        up = jnp.where(lane == 127, c, pltpu.roll(c, 127, 1))
        low = jnp.where(lane == 0, c, pltpu.roll(c, 1, 1))
        return c, east(f), west(f), here(f, 1), here(f, -1), up, low

    def lap(parts):
        c, e, w, n, s, up, low = parts
        return e + w + n + s + up + low - 6.0 * c

    def slopes(parts):
        c, e, w, n, s, up, low = parts
        return e - w, n - s, up - low

    pu, pv, pw = around(0), around(1), around(2)
    du, dv, dw = slopes(pu), slopes(pv), slopes(pw)
    strain = 2.0 * (du[0] * du[0] + dv[1] * dv[1] + dw[2] * dw[2])
    uv = du[1] + dv[0]
    uw = du[2] + dw[0]
    vw = dv[2] + dw[1]
    strain = strain + uv * uv + uw * uw + vw * vw
    visc = smag_coef * jnp.sqrt(0.25 * strain + epsilon)
    put(0, pu[0] + visc * lap(pu))
    put(1, pv[0] + visc * lap(pv))
    pb = around(3)
    put(2, pw[0] + visc * lap(pw) + buoyancy_coef * pb[0])
    fb = pb[0] + visc * lap(pb)
    put(3, fb)
    pq = around(4)
    fq = pq[0] + visc * lap(pq)
    put(4, fq)
    put(5, fq - 0.5 * fb)


def inner_kernel(state, new, buoy, vapour, sat, planes, fresh, in_sem, out_sem):
    nx, ny = state.shape[1], state.shape[2]
    inside = pl.ds(8, ny - 16)
    last = (buoy, vapour, sat)

    def fetch(x):
        return pltpu.make_async_copy(state.at[:, x], planes.at[:, x], in_sem.at[x])

    def store(x):
        return pltpu.make_async_copy(
            fresh.at[:, x, inside, :], new.at[pl.ds(0, 3), x, inside, :], out_sem.at[x]
        )

    for x in range(nx):
        fetch(x).start()
    fetch(0).wait()
    fetch(1).wait()

    def body(x, carry):
        fetch(x + 1).wait()
        for base in range(8, ny - 8, 8):

            def here(f, shift, base=base):
                return planes[f, x, base + shift : base + shift + 8, :]

            def west(f, base=base):
                return planes[f, x - 1, base : base + 8, :]

            def east(f, base=base):
                return planes[f, x + 1, base : base + 8, :]

            def put(f, value, base=base):
                if f >= 3:
                    last[f - 3][x, base : base + 8, :] = value
                else:
                    fresh[f, x, base : base + 8, :] = value

            step_rows(here, west, east, put)
        store(x).start()
        return carry

    lax.fori_loop(1, nx - 1, body, 0)
    for x in range(1, nx - 1):
        store(x).wait()


def edge_rows(planes, x, side, halo, west, east, put):
    ny = planes.shape[2]
    at = side * (ny - 8)
    sub = iota((8, 128), 0)

    def here(f, shift):
        if shift == 2 * side - 1:
            c = planes[f, x, at : at + 8, :]
            if side:
                return jnp.where(sub == 7, halo(f), pltpu.roll(c, 7, 0))
            return jnp.where(sub == 0, halo(f), pltpu.roll(c, 1, 0))
        return planes[f, x, at + shift : at + shift + 8, :]

    step_rows(here, lambda f: west(f, at), lambda f: east(f, at), put)


def ends_kernel(planes, south, north, new_in, b_in, q_in, s_in, new, buoy, vapour, sat, edges, out_sem):
    nx, ny = planes.shape[1], planes.shape[2]
    last = (buoy, vapour, sat)

    def step(x, carry):
        for side, ref in ((0, south), (1, north)):

            def put(f, value, side=side):
                if f >= 3:
                    last[f - 3][x, side * (ny - 8) : side * (ny - 8) + 8, :] = value
                else:
                    edges[side, f, x] = value

            edge_rows(
                planes,
                x,
                side,
                lambda f, ref=ref: ref[pl.ds(f * nx + x, 1), :],
                lambda f, at: planes[f, x - 1, at : at + 8, :],
                lambda f, at: planes[f, x + 1, at : at + 8, :],
                put,
            )
        return carry

    lax.fori_loop(1, nx - 1, step, 0, unroll=2)
    copies = [
        pltpu.make_async_copy(
            edges.at[side, :, pl.ds(1, nx - 2)],
            new.at[pl.ds(0, 3), pl.ds(1, nx - 2), pl.ds(side * (ny - 8), 8), :],
            out_sem.at[side],
        )
        for side in range(2)
    ]
    for copy in copies:
        copy.start()
    for copy in copies:
        copy.wait()


def rim_kernel(
    planes, left, right, south, north, new_in, b_in, q_in, s_in, new, buoy, vapour, sat, fresh, out_sem
):
    nx, ny = planes.shape[1], planes.shape[2]
    last = (buoy, vapour, sat)
    copies = []
    for side, x in ((0, 0), (1, nx - 1)):

        def inward(f, at, x=x, side=side):
            return planes[f, x + 1 - 2 * side, at : at + 8, :]

        def outward(f, at, side=side):
            ref = right if side else left
            return ref[f * ny + at : f * ny + at + 8, :]

        west, east = (inward, outward) if side else (outward, inward)
        for at in range(0, ny, 8):

            def put(f, value, at=at, x=x, side=side):
                if f >= 3:
                    last[f - 3][x, at : at + 8, :] = value
                else:
                    fresh[f, side, at : at + 8, :] = value

            if at in (0, ny - 8):
                ref = north if at else south
                edge_rows(
                    planes,
                    x,
                    1 if at else 0,
                    lambda f, ref=ref, x=x: ref[f * nx + x : f * nx + x + 1, :],
                    west,
                    east,
                    put,
                )
            else:
                step_rows(
                    lambda f, shift, x=x, at=at: planes[f, x, at + shift : at + shift + 8, :],
                    lambda f, at=at: west(f, at),
                    lambda f, at=at: east(f, at),
                    put,
                )
        copy = pltpu.make_async_copy(
            fresh.at[:, side], new.at[pl.ds(0, 3), x], out_sem.at[side]
        )
        copy.start()
        copies.append(copy)
    for copy in copies:
        copy.wait()


def inner_planes(state):
    _, nx, ny, nz = state.shape
    return pl.pallas_call(
        inner_kernel,
        out_shape=[pltpu.HBM(state.shape, f32)]
        + [pltpu.VMEM((nx, ny, nz), f32)] * 3
        + [pltpu.VMEM(state.shape, f32)],
        in_specs=[HBM],
        out_specs=[HBM] + [VMEM] * 4,
        scratch_shapes=[
            pltpu.VMEM((3, nx, ny, nz), f32),
            pltpu.SemaphoreType.DMA((nx,)),
            pltpu.SemaphoreType.DMA((nx,)),
        ],
        compiler_params=pltpu.CompilerParams(vmem_limit_bytes=16 << 20),
        cost_estimate=pl.CostEstimate(flops=60_000_000, bytes_accessed=36 << 20, transcendentals=0),
        name="inner",
    )(*in_hbm(state))


def edge_planes(kernel, planes, halos, fields, scratch, name):
    new, buoy = fields[:2]
    at = 1 + len(halos)
    return pl.pallas_call(
        kernel,
        out_shape=[pltpu.HBM(new.shape, f32)] + [pltpu.VMEM(buoy.shape, f32)] * 3,
        in_specs=[VMEM] * at + [HBM] + [VMEM] * 3,
        out_specs=[HBM] + [VMEM] * 3,
        input_output_aliases={at + i: i for i in range(4)},
        scratch_shapes=[scratch, pltpu.SemaphoreType.DMA((2,))],
        compiler_params=pltpu.CompilerParams(vmem_limit_bytes=8 << 20),
        cost_estimate=pl.CostEstimate(flops=8_000_000, bytes_accessed=9 << 20, transcendentals=0),
        name=name,
    )(planes, *halos, *fields)


SUMS = 2
GROUP = 32


def grow_codes(codes, cap, bufs, sat, totals, radius, near, mass, value_out, cols_v, cols_s, col_sem, rad_sem):
    count = len(codes)
    for i, (which, top, _) in enumerate(codes):
        at = top + 3 * cap
        cols_v[i : i + 1, :] = bufs[which][at : at + 1, :].astype(i32)
    get_cols = pltpu.make_async_copy(cols_v, cols_s, col_sem)
    get_cols.start()
    yield
    get_cols.wait()
    put_radius = []
    for i in range(count + 1):

        def rows(step, carry, i=i):
            for u in range(GROUP):
                j = step * GROUP + u
                if i < count:
                    near[i % 2][pl.ds(j, 1), :] = sat[pl.ds(cols_s[i, j], 1), :]
                if i > 0:
                    totals[u % SUMS][pl.ds(cols_s[i - 1, j], 1), :] += mass[(i - 1) % 2][pl.ds(j, 1), :]
            return carry

        lax.fori_loop(0, cap // GROUP, rows, 0)
        if i == count:
            break
        which, top, slot = codes[i]
        ref = bufs[which]
        for at in range(0, cap, 8):
            rad = ref[top + at : top + at + 8, :]
            sol = ref[top + cap + at : top + cap + at + 8, :]
            mul = ref[top + 2 * cap + at : top + 2 * cap + at + 8, :]
            alive = mul > 0.0
            start = jnp.where(alive, rad, 1.0)
            square = start * start
            base = square + growth_coef * near[i % 2][at : at + 8, :]
            sol = (growth_coef * solute_coef) * sol
            inv = 1.0 / start
            for _ in range(ITERS):
                inside = base + inv * (sol * (inv * inv) - growth_coef * curvature_coef)
                inside = jnp.maximum(inside, floor_square)
                inv = lax.rsqrt(inside)
            value = inside * inv
            value_out[i * cap + at : i * cap + at + 8, :] = jnp.where(alive, value, 0.0)
            mass[i % 2][at : at + 8, :] = mul * (value * inside - start * square)
        copy = pltpu.make_async_copy(
            value_out.at[pl.ds(i * cap, cap), :],
            radius.at[pl.ds(slot * cap, cap), :],
            rad_sem.at[i],
        )
        copy.start()
        put_radius.append(copy)
    yield
    for copy in put_radius:
        copy.wait()


def early_kernel(codes, cap, n, *refs):
    bufs, sat = refs[:n], refs[n]
    radius = refs[n + 1]
    totals = refs[n + 2 : n + 2 + SUMS]
    near0, near1, mass0, mass1, *rest = refs[n + 2 + SUMS :]
    steps = grow_codes(codes, cap, bufs, sat, totals, radius, (near0, near1), (mass0, mass1), *rest)
    next(steps)
    for total in totals:
        total[...] = jnp.zeros_like(total)
    for _ in steps:
        pass


def late_kernel(codes, cap, n, *refs):
    bufs, sat, buoy, vapour = refs[:n], refs[n], refs[n + 1], refs[n + 2]
    refs = refs[n + 3 + SUMS + 2 :]
    radius, new = refs[:2]
    totals = refs[2 : 2 + SUMS]
    near0, near1, mass0, mass1, *rest, fields, out_sem = refs[2 + SUMS :]
    nx, ny = new.shape[1], new.shape[2]
    steps = grow_codes(codes, cap, bufs, sat, totals, radius, (near0, near1), (mass0, mass1), *rest)
    next(steps)
    next(steps)

    def put(x):
        return pltpu.make_async_copy(fields.at[:, x], new.at[pl.ds(3, 2), x], out_sem.at[x])

    def final(x, carry):
        for at in range(0, ny, 8):
            tot = totals[0][pl.ds(x * ny + at, 8), :]
            for total in totals[1:]:
                tot = tot + total[pl.ds(x * ny + at, 8), :]
            fields[0, x, at : at + 8, :] = buoy[x, at : at + 8, :] + latent_coef * tot
            fields[1, x, at : at + 8, :] = vapour[x, at : at + 8, :] - condense_coef * tot
        put(x).start()
        return carry

    lax.fori_loop(0, nx, final, 0)
    for _ in steps:
        pass
    for x in range(nx):
        put(x).wait()


def grow_scratch(count, cap, nz):
    return [pltpu.VMEM((cap, nz), f32)] * 4 + [
        pltpu.VMEM((count * cap, nz), f32),
        pltpu.VMEM((8, 128), i32),
        pltpu.SMEM((8, 128), i32),
        pltpu.SemaphoreType.DMA,
        pltpu.SemaphoreType.DMA((count,)),
    ]


def grow_early(bufs, codes, cap, sat):
    cells, nz = sat.shape
    n, count = len(bufs), len(codes)
    return pl.pallas_call(
        functools.partial(early_kernel, codes, cap, n),
        out_shape=[pltpu.HBM((CODES * cap, nz), f32)] + [pltpu.VMEM((cells, nz), f32)] * SUMS,
        in_specs=[VMEM] * (n + 1),
        out_specs=[HBM] + [VMEM] * SUMS,
        scratch_shapes=grow_scratch(count, cap, nz),
        compiler_params=pltpu.CompilerParams(vmem_limit_bytes=8 << 20),
        cost_estimate=pl.CostEstimate(flops=20_000_000, bytes_accessed=16 << 20, transcendentals=0),
        name="early",
    )(*bufs, sat)


def grow_late(bufs, codes, cap, sat, buoy, vapour, totals, new, radius):
    cells, nz = sat.shape
    _, nx, ny, _ = new.shape
    n, count = len(bufs), len(codes)
    at = n + 3
    return pl.pallas_call(
        functools.partial(late_kernel, codes, cap, n),
        out_shape=[pltpu.HBM(radius.shape, f32), pltpu.HBM(new.shape, f32)]
        + [pltpu.VMEM((cells, nz), f32)] * SUMS,
        in_specs=[VMEM] * (at + SUMS) + [HBM] * 2,
        out_specs=[HBM] * 2 + [VMEM] * SUMS,
        input_output_aliases={at + i: 2 + i for i in range(SUMS)}
        | {at + SUMS: 1, at + SUMS + 1: 0},
        scratch_shapes=grow_scratch(count, cap, nz)
        + [pltpu.VMEM((2, nx, ny, nz), f32), pltpu.SemaphoreType.DMA((nx,))],
        compiler_params=pltpu.CompilerParams(vmem_limit_bytes=12 << 20),
        cost_estimate=pl.CostEstimate(flops=20_000_000, bytes_accessed=16 << 20, transcendentals=0),
        name="late",
    )(*bufs, sat, buoy, vapour, *totals, new, radius)[:2]


def moved(value, dx, dy):
    nx, ny = lax.axis_size("gx"), lax.axis_size("gy")
    pairs = [
        (tx * ny + ty, (tx + dx) % nx * ny + (ty + dy) % ny) for tx in range(nx) for ty in range(ny)
    ]
    return lax.ppermute(value, ("gx", "gy"), pairs)


def on_device(state, radius, solute, multiplicity, block_column, destination, live_blocks):
    _, nx, ny, nz = state.shape
    cap = radius.shape[0] // 8
    one = parcel_rows(cap)
    *sides, own = pack_blocks(
        radius, solute, multiplicity, block_column, destination, live_blocks, state
    )
    first = [moved(side, dx, dy) for side, (dx, dy, _, _) in zip(sides, FIRST)]
    *fields, planes = inner_planes(state)
    along_x, along_y = first[:2], first[2:]
    along_y, fields, planes = lax.optimization_barrier((along_y, fields, planes))
    from_north, from_south = along_y
    scratch = pltpu.VMEM((2, 3, nx, 8, nz), f32)
    fields = edge_planes(ends_kernel, planes, [from_south, from_north], fields, scratch, "ends")
    along_x, fields = lax.optimization_barrier((along_x, fields))
    first = [*along_x, *along_y]
    from_right, from_left = along_x
    tops = (5 * ny, 5 * ny, 5 * nx, 5 * nx)
    second = [
        moved(side[top + one : top + 2 * one], dx, dy)
        for side, top, (dx, dy, _) in zip(first, tops, SECOND)
    ]
    scratch = pltpu.VMEM((3, 2, ny, nz), f32)
    halos = [from_left, from_right, from_south, from_north]
    new, buoy, vapour, sat = edge_planes(rim_kernel, planes, halos, fields, scratch, "rim")
    sat = sat.reshape(nx * ny, nz)
    codes = ((0, 0, OWN),) + tuple(
        (1 + i, top, end) for i, (top, (_, _, end, _)) in enumerate(zip(tops, FIRST))
    )
    value, *totals = grow_early([own] + first, codes, cap, sat)
    codes = tuple((i, 0, code) for i, (_, _, code) in enumerate(SECOND))
    value, new = grow_late(second, codes, cap, sat, buoy, vapour, totals, new, value)
    return new, value


def solution(mesh):
    placed = (
        P(None, "gx", "gy", None),
        P(("gx", "gy"), None),
        P(("gx", "gy"), None),
        P(("gx", "gy"), None),
        P(("gx", "gy")),
        P(("gx", "gy"), None),
        P(("gx", "gy")),
    )
    return jax.shard_map(
        on_device,
        mesh=mesh,
        in_specs=placed,
        out_specs=(P(None, "gx", "gy", None), P(("gx", "gy"), None)),
        check_vma=False,
    )
```
